32 devices in a mesh: dp: 2 (over y), owner: 16 (over z, x, core).
Axes of the slice: x: 2, y: 2, z: 4, core: 2. Of those that a mesh axis runs over, the one named last changes fastest.
Arguments:
- partials: bfloat16 [32, 48, 128, 128], P(('dp', 'owner')), may hold values from -1.25 to 1.25
- owners: int32 [48], replicated, may hold values from 0 to 15, as said below
- step_count: int32 [1], replicated, may hold values from 1 to 49
- master: float32 [96, 128, 128], P('owner'), may hold values from -0.3125 to 0.3125
- moment: float32 [96, 128, 128], P('owner'), may hold values from -4 to 4
- second: float32 [96, 128, 128], P('owner'), may hold values from 0.1 to 10
- stat_left: float32 [96, 128, 128], P('owner'), may hold values from -1.5 to 82
- stat_right: float32 [96, 128, 128], P('owner'), may hold values from -1.5 to 82
- basis_left: float32 [96, 128, 128], P('owner'), may hold values from -0.12 to 1.12
- basis_right: float32 [96, 128, 128], P('owner'), may hold values from -0.12 to 1.12
Outputs:
- weights_all: bfloat16 [48, 128, 128], replicated
- direction: float32 [96, 128, 128], P('owner')
- left_new: float32 [96, 128, 128], P('owner')
- right_new: float32 [96, 128, 128], P('owner')
The draws below stay inside these ranges and needn't reach their ends.
Inputs may be any that keep to these rules, and one draw needn't show every extreme that they name: `owners`: each owner index is named by at least one and at most 6 blocks, and some index by exactly 6.
All inputs are finite; a program needn't handle non-finite values.
Results may differ from the reference program's by a relative error of at most 0.0065.
Values may be sent and summed in bfloat16 or wider, within the bound.
No kernel may reach another device: no remote copies, remote signals or barrier semaphores. Data moves between devices by JAX's collectives and lax.ppermute only.
A program may use at most 128 MiB of HBM per device.

```python
import math
import jax
import jax.numpy as jnp
from jax import lax

B = 128
OWNER_SLOTS = 6
NS_ITERS = 6
TOTAL_SLOTS = 96
BLOCKS = 48
SOURCES = 32
N_OWNER = 16


def statistic(key, salt):
    key_noise, key_diag = jax.random.split(jax.random.fold_in(key, salt))
    total_slot_count = OWNER_SLOTS * N_OWNER
    jitter = jax.random.uniform(key_noise, (total_slot_count, B, B), jnp.float32, -1.0, 1.0)
    diagonal = jnp.exp(jax.random.uniform(key_diag, (total_slot_count, B), jnp.float32, math.log(4.0), math.log(40.0)))
    symmetric = 0.5 * (jitter + jnp.swapaxes(jitter, 1, 2))
    return symmetric + diagonal[:, :, None] * jnp.eye(B, dtype=jnp.float32)[None, :, :]


def near_identity(key, salt):
    key_noise = jax.random.fold_in(key, salt)
    total_slot_count = OWNER_SLOTS * N_OWNER
    jitter = jax.random.uniform(key_noise, (total_slot_count, B, B), jnp.float32, -0.06, 0.06)
    return jitter + jnp.eye(B, dtype=jnp.float32)[None, :, :]


def draw_stat_left(key, part):
    return statistic(key, 3)


def draw_stat_right(key, part):
    return statistic(key, 5)


def draw_basis_left(key, part):
    return near_identity(key, 7)


def draw_basis_right(key, part):
    return near_identity(key, 9)


def draw_owners(key, part):
    key_order, key_first, key_shuffle = jax.random.split(jax.random.fold_in(key, 11), 3)
    total_slot_count = N_OWNER * OWNER_SLOTS
    owner_scores = jax.random.permutation(key_order, total_slot_count).astype(jnp.int32)
    busiest_owner = jax.random.randint(key_first, (), 0, N_OWNER)
    slot_position = jnp.arange(total_slot_count, dtype=jnp.int32)
    extra_credit = jnp.where(slot_position // OWNER_SLOTS == busiest_owner, 2 * total_slot_count, jnp.where(slot_position % OWNER_SLOTS == 0, total_slot_count, 0))
    owner_scores = owner_scores + extra_credit.astype(jnp.int32)
    chosen = jnp.argsort(-owner_scores)[:OWNER_SLOTS * N_OWNER // 2]
    chosen = jax.random.permutation(key_shuffle, chosen)
    return (chosen // OWNER_SLOTS).astype(jnp.int32)


def strengthened(values, own_key, source, target, shards_of, factor):
    owner, partner = [(jnp.arange(values.shape[position]) // (values.shape[position] // shards_of)).reshape([-1 if axis == position else 1 for axis in range(values.ndim)]) for position in (source, target)]
    chosen = jax.random.permutation(own_key, shards_of)[partner]
    strong = (owner == chosen) | (owner == (partner + shards_of // 2) % shards_of)
    return jnp.where(strong, factor * values, values)


def level_of(key, shape, shards, smallest, largest):
    gain = 1.0
    for axis_at, parts in shards:
        draws = jax.random.uniform(jax.random.fold_in(jax.random.fold_in(key, 6), axis_at), (parts,), jnp.float32, smallest / len(shards), largest / len(shards))
        gain = gain * jnp.repeat(jnp.exp(draws), shape[axis_at] // parts).reshape((-1,) + (1,) * (len(shape) - 1 - axis_at))
    return gain


def gaussian(key, dims, scale, most, cuts=(), held_as=jnp.bfloat16):
    entries = scale * jax.random.normal(key, dims, jnp.float32)
    if cuts:
        entries = entries * level_of(key, dims, cuts, -0.22, 0.18)
    return jnp.clip(entries, -most, most).astype(held_as)


def bell_draw_with(key, extent, spread, most, cuts, heavy, kind=jnp.bfloat16):
    result = spread * jax.random.normal(key, extent, jnp.float32)
    if cuts:
        result = result * level_of(key, extent, cuts, -0.22, 0.18)
    return jnp.clip(strengthened(result, jax.random.fold_in(key, 3), *heavy), -most, most).astype(kind)


def setup_inputs(seed: int = 0) -> dict:
    key_of = jax.random.split(jax.random.key(seed), 11)
    return {
        "partials": bell_draw_with(key_of[0], (SOURCES, BLOCKS, B, B), 0.0625, 1.25, ((0, 32),), (0, 1, 16, 2.0)),
        "owners": draw_owners(jax.random.fold_in(key_of[10], 71), 0),
        "step_count": jax.random.randint(key_of[2], (1,), 1, 50).astype(jnp.int32),
        "master": gaussian(key_of[3], (TOTAL_SLOTS, B, B), 0.02, 0.3125, ((0, 16),), jnp.float32),
        "moment": gaussian(key_of[4], (TOTAL_SLOTS, B, B), 0.3, 4.0, ((0, 16),), jnp.float32),
        "second": jnp.clip(jnp.exp(math.log(10.0) - 4.6051702 * jax.random.uniform(key_of[5], (TOTAL_SLOTS, B, B), jnp.float32) ** level_of(key_of[5], (TOTAL_SLOTS, B, B), ((0, 16),), -0.2, 0.2)), 0.1, 10.0),
        "stat_left": draw_stat_left(jax.random.fold_in(key_of[10], 71), 0),
        "stat_right": draw_stat_right(jax.random.fold_in(key_of[10], 71), 0),
        "basis_left": draw_basis_left(jax.random.fold_in(key_of[10], 71), 0),
        "basis_right": draw_basis_right(jax.random.fold_in(key_of[10], 71), 0),
    }


def product(left, right):
    return jnp.matmul(left, right, precision=lax.Precision.HIGHEST)

def transposed(array):
    return jnp.swapaxes(array, 1, 2)

def refresh(stat, basis):
    power = product(stat, basis)
    magnitude = jnp.sqrt(lax.optimization_barrier(jnp.sum(power * power, axis=(1, 2), keepdims=True)))
    iterate = power / (magnitude + 1e-06)
    for repeat_count in range(NS_ITERS):
        iterate = 1.5 * iterate - 0.5 * product(iterate, product(transposed(iterate), iterate))
    return iterate

def slot_layout(owners, slot_count, total_slot_count):
    block_count = owners.shape[0]
    slot_position = jnp.arange(block_count, dtype=jnp.int32)
    before = (owners[:, None] == owners[None, :]) & (slot_position[:, None] > slot_position[None, :])
    rank_in = lax.optimization_barrier(jnp.sum(before.astype(jnp.int32), axis=1))
    target = owners * slot_count + rank_in
    matches = (target[:, None] == jnp.arange(total_slot_count, dtype=jnp.int32)[None, :]).astype(jnp.int32)
    source = lax.optimization_barrier(jnp.sum(matches * slot_position[:, None], axis=0))
    occupied = lax.optimization_barrier(jnp.sum(matches, axis=0))
    return (target, source, occupied)

def soap_update(gradient, occupied, moment, second, stat_left, stat_right, basis_left, basis_right, step_count):
    elapsed = step_count[0].astype(jnp.float32)
    moment_new = 0.95 * moment + 0.05 * gradient
    rotated = product(transposed(basis_left), product(gradient, basis_right))
    rot_moment = product(transposed(basis_left), product(moment_new, basis_right))
    second_new = 0.95 * second + 0.05 * rotated * rotated
    correction = 1.0 - jnp.power(jnp.float32(0.95), elapsed)
    scaled = rot_moment / correction / (jnp.sqrt(second_new / correction) + 1e-08)
    occupied_mask = (occupied > 0)[:, None, None]
    direction = jnp.where(occupied_mask, product(basis_left, product(scaled, transposed(basis_right))), 0.0)
    left_stat = 0.95 * stat_left + 0.05 * product(gradient, transposed(gradient))
    right_stat = 0.95 * stat_right + 0.05 * product(transposed(gradient), gradient)
    left_new = jnp.where(occupied_mask, refresh(left_stat, basis_left), basis_left)
    right_new = jnp.where(occupied_mask, refresh(right_stat, basis_right), basis_right)
    return (direction, left_new, right_new)

def reference(partials, owners, step_count, master, moment, second, stat_left, stat_right, basis_left, basis_right):
    total_slot_count = OWNER_SLOTS * N_OWNER

    def accumulate(running, piece):
        return (running + piece.astype(jnp.float32), None)
    grad_sum = lax.scan(accumulate, jnp.zeros(partials.shape[1:], jnp.float32), partials)[0]
    target, source, occupied = slot_layout(owners, OWNER_SLOTS, total_slot_count)
    gradient = jnp.take(grad_sum, source, axis=0) * (occupied > 0).astype(jnp.float32)[:, None, None]
    direction, left_new, right_new = soap_update(gradient, occupied, moment, second, stat_left, stat_right, basis_left, basis_right, step_count)
    updated = (master - 0.01 * (direction + 0.1 * master)).astype(jnp.bfloat16)
    weights_all = jnp.take(updated, target, axis=0)
    return (weights_all, direction, left_new, right_new)
```

```python
import functools

import jax
import jax.numpy as jnp
from jax import lax
from jax.experimental import pallas as pl
from jax.experimental.pallas import tpu as pltpu
from jax.sharding import PartitionSpec as P

NS_ITERS = 6
AXES = ("dp", "owner")
F32 = jnp.float32
BF16 = jnp.bfloat16
VMEM_LIMIT = 48 * 1024 * 1024
VMEM = pl.BlockSpec(memory_space=pltpu.VMEM)
SMEM = pl.BlockSpec(memory_space=pltpu.SMEM)


def shape(dims, dtype):
    return jax.ShapeDtypeStruct(dims, dtype)


def call(kernel, scalars, arrays, outs, flops=0):
    moved = sum(a.size * a.dtype.itemsize for a in list(arrays) + list(outs))
    return pl.pallas_call(
        kernel,
        out_shape=tuple(outs),
        in_specs=[SMEM] * len(scalars) + [VMEM] * len(arrays),
        out_specs=tuple(VMEM for _ in outs),
        compiler_params=pltpu.CompilerParams(vmem_limit_bytes=VMEM_LIMIT),
        cost_estimate=pl.CostEstimate(flops=flops, bytes_accessed=moved, transcendentals=0),
    )(*scalars, *arrays)


class Grid:
    def __init__(self, dp_count, owner_count):
        self.dp, self.core = dp_count, 2
        self.high = 4
        self.middle = owner_count // (self.core * self.high)
        self.owners = owner_count

    def place(self):
        owner = lax.axis_index("owner")
        return jnp.stack(
            [
                lax.axis_index("dp"),
                owner // (self.core * self.middle),
                owner // self.core % self.middle,
                owner % self.core,
            ]
        ).astype(jnp.int32)

    def swap(self, array, dp=0, high=0, middle=0, core=0):
        step = (high * self.middle + middle) * self.core + core
        pairs = [
            (d * self.owners + o, (d ^ dp) * self.owners + (o ^ step))
            for d in range(self.dp)
            for o in range(self.owners)
        ]
        return lax.ppermute(array, AXES, pairs)


def split(value):
    top = value.astype(BF16)
    return top, (value - top.astype(F32)).astype(BF16)


def dot(left, right, dims):
    return lax.dot_general(left, right, (dims, ((), ())), preferred_element_type=F32)


NN = ((1,), (0,))
NT = ((1,), (1,))
TN = ((0,), (0,))


def product(left, right, dims=NN):
    (left_top, left_low), (right_top, right_low) = left, right
    small = dot(left_low, right_top, dims) + dot(left_top, right_low, dims)
    return dot(left_top, right_top, dims) + small


def spread_kernel(grid, slots, place, owners, rank, own, other, *outs):
    rows = own.shape[1] // grid.dp
    dp, middle, core = place[0], place[2], place[3]

    def step(block, carry):
        owner = owners[block]
        high_of = owner // (grid.core * grid.middle)
        middle_of = owner // grid.core % grid.middle
        at = high_of * slots + rank[block]

        @pl.when(owner % grid.core == core)
        def _():
            for dm in range(grid.middle):

                @pl.when(middle_of == middle ^ dm)
                def _():
                    for dd in range(grid.dp):
                        part = pl.ds(pl.multiple_of((dp ^ dd) * rows, rows), rows)
                        total = own[block, part].astype(F32) + other[block, part].astype(F32)
                        outs[dm * grid.dp + dd][at] = total.astype(BF16)

        return carry

    lax.fori_loop(0, own.shape[0], step, 0)


def gather_sum_kernel(grid, slots, place, *refs):
    count = grid.middle * grid.dp
    arrays, outs = refs[:count], refs[count:]
    for dh in range(grid.high):
        first = (place[1] ^ dh) * slots
        for slot in range(slots):
            total = arrays[0][first + slot].astype(F32)
            for array in arrays[1:]:
                total = total + array[first + slot].astype(F32)
            outs[dh][slot] = total.astype(BF16)


def sum_kernel(*refs):
    arrays, out = refs[:-1], refs[-1]
    for slot in range(out.shape[0]):
        total = arrays[0][slot].astype(F32)
        for array in arrays[1:]:
            total = total + array[slot].astype(F32)
        out[slot] = total.astype(BF16)


def moment_kernel(moment, left, right, out):
    for slot in range(out.shape[0]):
        half = product(split(moment[slot]), split(right[slot]))
        out[slot] = product(split(left[slot]), split(half), TN)


def step_kernel(grid, place, held, correction, *refs):
    parts = refs[: grid.dp]
    rot_old, second, master, left, right, gradient, direction, updated = refs[grid.dp :]
    slots, rows = parts[0].shape[:2]
    dp = place[0]
    c = correction[0]
    for dd in range(grid.dp):
        part = pl.ds(pl.multiple_of((dp ^ dd) * rows, rows), rows)
        gradient[:, part, :] = parts[dd][...]
    mine = pl.ds(pl.multiple_of(dp * rows, rows), rows)
    for slot in range(slots):
        live = slot < held[0]
        right_top, right_low = split(right[slot])
        left_parts = split(left[slot])
        half = dot(gradient[slot], right_top, NN) + dot(gradient[slot], right_low, NN)
        rotated = product(left_parts, split(half), TN)
        rot_moment = 0.95 * rot_old[slot] + 0.05 * rotated
        second_new = 0.95 * second[slot] + 0.05 * rotated * rotated
        scaled = rot_moment / c / (jnp.sqrt(second_new / c) + 1e-08)
        turned = product(split(scaled), (right_top, right_low), NT)
        moved = product(left_parts, split(turned))
        direction[slot] = jnp.where(live, moved, 0.0)
        weights = master[slot, mine]
        updated[slot] = (weights - 0.01 * (direction[slot, mine] + 0.1 * weights)).astype(BF16)


def refresh_kernel(dims, held, gradient, stat, basis, out):
    slots = out.shape[0]
    for slot in range(slots):
        gram = dot(gradient[slot], gradient[slot], dims)
        power = product(split(0.95 * stat[slot] + 0.05 * gram), split(basis[slot]))
        out[slot] = power / (jnp.sqrt(jnp.sum(power * power)) + 1e-06)

    def step(_, carry):
        for slot in range(slots):
            iterate = out[slot]
            parts = split(iterate)
            square = product(parts, parts, TN)
            out[slot] = 1.5 * iterate - 0.5 * product(parts, split(square))
        return carry

    lax.fori_loop(0, NS_ITERS, step, 0)
    for slot in range(slots):
        out[slot] = jnp.where(slot < held[0], out[slot], basis[slot])


def join_kernel(grid, place, *refs):
    arrays, out = refs[:-1], refs[-1]
    slots = arrays[0].shape[0]
    for dh in range(grid.high):
        first = (place[1] ^ dh) * slots
        for slot in range(slots):
            out[first + slot] = arrays[dh][slot]


def weights_kernel(grid, slots, place, owners, rank, *refs):
    arrays, out = refs[:-1], refs[-1]
    rows = arrays[0].shape[1]
    dp, middle, core = place[0], place[2], place[3]

    def step(block, carry):
        owner = owners[block]
        at = owner // (grid.core * grid.middle) * slots + rank[block]
        for dc in range(grid.core):
            for dm in range(grid.middle):
                from_core = owner % grid.core == core ^ dc
                from_middle = owner // grid.core % grid.middle == middle ^ dm

                @pl.when(from_core & from_middle)
                def _():
                    for dd in range(grid.dp):
                        part = pl.ds(pl.multiple_of((dp ^ dd) * rows, rows), rows)
                        out[block, part] = arrays[(dc * grid.middle + dm) * grid.dp + dd][at]

        return carry

    lax.fori_loop(0, out.shape[0], step, 0)


def body(
    partials,
    owners,
    step_count,
    master,
    moment,
    second,
    stat_left,
    stat_right,
    basis_left,
    basis_right,
):
    grid = Grid(lax.axis_size("dp"), lax.axis_size("owner"))
    slots, size = master.shape[:2]
    blocks = owners.shape[0]
    rows = size // grid.dp
    place = grid.place()
    position = jnp.arange(blocks, dtype=jnp.int32)
    earlier = (owners[:, None] == owners[None, :]) & (position[:, None] > position[None, :])
    rank = jnp.sum(earlier.astype(jnp.int32), axis=1)
    held = jnp.sum((owners == lax.axis_index("owner")).astype(jnp.int32))[None]
    correction = 1.0 - jnp.power(jnp.float32(0.95), step_count.astype(F32))

    share = shape((slots, rows, size), BF16)
    column = shape((grid.high * slots, rows, size), BF16)
    state = shape((slots, size, size), F32)
    plane = [(dm, dd) for dm in range(grid.middle) for dd in range(grid.dp)]

    own = partials[0]
    other = grid.swap(own, core=1)
    sent = call(
        functools.partial(spread_kernel, grid, slots),
        (place, owners, rank),
        (own, other),
        [column] * len(plane),
    )
    got = [sent[0]] + [
        grid.swap(a, middle=dm, dp=dd) for a, (dm, dd) in zip(sent[1:], plane[1:], strict=True)
    ]
    (rot_old,) = call(moment_kernel, (), (moment, basis_left, basis_right), [state], 12 * slots * size**3)
    sent = call(
        functools.partial(gather_sum_kernel, grid, slots), (place,), got, [share] * grid.high
    )
    got = [sent[0]] + [grid.swap(sent[dh], high=dh) for dh in range(1, grid.high)]
    (summed,) = call(sum_kernel, (), got, [share])
    parts = [summed] + [grid.swap(summed, dp=dd) for dd in range(1, grid.dp)]
    gradient, direction, updated = call(
        functools.partial(step_kernel, grid),
        (place, held, correction),
        (*parts, rot_old, second, master, basis_left, basis_right),
        [shape((slots, size, size), BF16), state, share],
        22 * slots * size**3,
    )
    cost = 2 * (1 + 3 + 36) * slots * size**3
    (left_new,) = call(
        functools.partial(refresh_kernel, NT), (held,), (gradient, stat_left, basis_left), [state], cost
    )
    (right_new,) = call(
        functools.partial(refresh_kernel, TN), (held,), (gradient, stat_right, basis_right), [state], cost
    )
    got = [updated] + [grid.swap(updated, high=dh) for dh in range(1, grid.high)]
    (joined,) = call(functools.partial(join_kernel, grid), (place,), got, [column])
    got = [joined] + [grid.swap(joined, middle=dm, dp=dd) for dm, dd in plane[1:]]
    got = got + [grid.swap(a, core=1) for a in got]
    (weights_all,) = call(
        functools.partial(weights_kernel, grid, slots),
        (place, owners, rank),
        got,
        [shape((blocks, size, size), BF16)],
    )
    return (weights_all, direction, left_new, right_new)


def solution(mesh):
    placed = (
        P(("dp", "owner"), None, None, None),
        P(),
        P(),
        P("owner", None, None),
        P("owner", None, None),
        P("owner", None, None),
        P("owner", None, None),
        P("owner", None, None),
        P("owner", None, None),
        P("owner", None, None),
    )
    return jax.shard_map(
        body,
        mesh=mesh,
        in_specs=placed,
        out_specs=(P(), P("owner", None, None), P("owner", None, None), P("owner", None, None)),
        check_vma=False,
    )
```

```python
import functools
import math

import jax
import jax.numpy as jnp
from jax import lax
from jax.experimental import pallas as pl
from jax.experimental.pallas import tpu as pltpu
from jax.sharding import PartitionSpec as P

NS_ITERS = 6
AXES = ("dp", "owner")
F32 = jnp.float32
BF16 = jnp.bfloat16
VMEM_LIMIT = 48 * 1024 * 1024
VMEM = pl.BlockSpec(memory_space=pltpu.VMEM)
SMEM = pl.BlockSpec(memory_space=pltpu.SMEM)
HBM = pl.BlockSpec(memory_space=pltpu.HBM)


def shape(dims, dtype):
    return jax.ShapeDtypeStruct(dims, dtype)


class Chain:
    def __init__(self):
        self.token = None

    def call(self, kernel, scalars, arrays, outs, flops=0, scratch=(), specs=None, moved=0):
        moved = moved or sum(a.size * a.dtype.itemsize for a in list(arrays) + list(outs))
        count = len(scalars) + len(arrays)
        tokens = () if self.token is None else (self.token,)
        specs = specs or [VMEM] * len(outs)

        def run(*refs):
            refs = list(refs)
            token = refs.pop(count + len(tokens) + len(outs))
            kernel(*refs[:count], *refs[count + len(tokens) :])
            token[...] = jnp.zeros_like(token)

        *results, self.token = pl.pallas_call(
            run,
            out_shape=(*outs, shape((8, 128), F32)),
            in_specs=[SMEM] * len(scalars)
            + [VMEM] * len(arrays)
            + [VMEM] * len(tokens),
            out_specs=(*specs, VMEM),
            scratch_shapes=list(scratch),
            compiler_params=pltpu.CompilerParams(vmem_limit_bytes=VMEM_LIMIT),
            cost_estimate=pl.CostEstimate(flops=flops, bytes_accessed=moved, transcendentals=0),
        )(*scalars, *arrays, *tokens)
        return results


class Grid:
    def __init__(self, dp_count, owner_count):
        self.dp, self.core = dp_count, 2
        self.high = 4
        self.middle = owner_count // (self.core * self.high)
        self.owners = owner_count

    def place(self):
        owner = lax.axis_index("owner")
        return jnp.stack(
            [
                lax.axis_index("dp"),
                owner // (self.core * self.middle),
                owner // self.core % self.middle,
                owner % self.core,
            ]
        ).astype(jnp.int32)

    def swap(self, array, dp=0, high=0, middle=0, core=0):
        step = (high * self.middle + middle) * self.core + core
        pairs = [
            (d * self.owners + o, (d ^ dp) * self.owners + (o ^ step))
            for d in range(self.dp)
            for o in range(self.owners)
        ]
        return lax.ppermute(array, AXES, pairs)


def split(value):
    top = value.astype(BF16)
    return top, (value - top.astype(F32)).astype(BF16)


def dot(left, right, dims):
    return lax.dot_general(left, right, (dims, ((), ())), preferred_element_type=F32)


NN = ((1,), (0,))
NT = ((1,), (1,))
TN = ((0,), (0,))


def as_left(value, axis=1):
    return jnp.concatenate(split(value), axis)


def as_right(value):
    half = jnp.concatenate(split(value), 1)
    return jnp.concatenate([half, half], 0)


def product(left, right, dims=NN):
    wide = dot(left, right, dims)
    size = wide.shape[1] // 2
    return wide[:, :size] + wide[:, size:]


def log2(count):
    return count.bit_length() - 1


class Table:
    def __init__(self, grid, slots):
        self.columns = grid.middle * grid.core
        self.groups = math.gcd(slots, grid.dp)
        self.shares = grid.dp // self.groups
        self.each = slots // self.groups
        self.length = grid.high * self.each
        self.rooms = (self.length * 2 // 3, self.length * 3 // 4, self.length)
        self.listed = 0
        self.counts = self.columns * self.groups * self.length
        self.inverse = self.counts + self.columns * self.groups
        self.held = self.inverse + self.length
        self.place = self.held + 1
        self.size = self.place + 4

    def slot(self, info, group, index):
        turn = group + self.groups - lax.rem(info[self.place + 1], self.groups)
        return self.groups * index + lax.rem(turn, self.groups)


def table_kernel(grid, table, place, owners, out, level, seen):
    for owner in range(grid.owners):
        seen[owner] = 0
    for part in range(table.columns * table.groups):
        out[table.counts + part] = 0
    for at in range(table.length):
        out[table.inverse + at] = -1
    column_mine = place[2] * grid.core + place[3]
    mine = column_mine * table.groups + lax.div(place[0], table.shares)

    def step(block, carry):
        owner = owners[block]
        rank = seen[owner]
        seen[owner] = rank + 1
        column, high = owner & (table.columns - 1), owner >> log2(table.columns)
        group, index = (rank + high) & (table.groups - 1), rank >> log2(table.groups)
        part = column * table.groups + group
        at = out[table.counts + part]
        out[table.counts + part] = at + 1
        out[table.listed + part * table.length + at] = block

        @pl.when(part == mine)
        def _():
            out[table.inverse + high * table.each + index] = at

        return carry

    lax.fori_loop(0, owners.shape[0], step, 0, unroll=8)
    out[table.held] = seen[place[1] * table.columns + column_mine]
    most = out[table.counts]
    for part in range(1, table.columns * table.groups):
        most = jnp.maximum(most, out[table.counts + part])
    level[0] = sum((most > room).astype(jnp.int32) for room in table.rooms[:-1])
    for at in range(4):
        out[table.place + at] = place[at]


def part_of(grid, table, info, dc, dm, dd):
    column = (info[table.place + 2] ^ dm) * grid.core + (info[table.place + 3] ^ dc)
    dp = info[table.place] ^ dd
    part = column * table.groups + lax.div(dp, table.shares)
    return info[table.counts + part], table.listed + part * table.length, lax.rem(dp, table.shares)


def copy_kernel(source, out):
    out[...] = source[...]


def spread_kernel(grid, table, info, own, other, *outs):
    rows = own.shape[1] // table.shares
    for dm in range(grid.middle):
        for dd in range(grid.dp):
            count, first, share = part_of(grid, table, info, 0, dm, dd)
            part = pl.ds(pl.multiple_of(share * rows, rows), rows)

            def put(out, at, carry):
                block = info[first + at]
                total = own[block, part].astype(F32) + other[block, part].astype(F32)
                out[at] = total.astype(BF16)
                return carry

            lax.fori_loop(0, count, functools.partial(put, outs[dm * grid.dp + dd]), 0)


def total_of(arrays, at):
    total = arrays[0][at].astype(F32)
    for array in arrays[1:]:
        total = total + array[at].astype(F32)
    return total.astype(BF16)


def gather_sum_kernel(grid, table, info, *refs):
    count = grid.middle * grid.dp
    arrays, outs = refs[:count], refs[count:]
    for dh in range(grid.high):
        first = table.inverse + (info[table.place + 1] ^ dh) * table.each
        for index in range(table.each):
            at = jnp.clip(info[first + index], 0, arrays[0].shape[0] - 1)
            outs[dh][index] = total_of(arrays, at)


def sum_kernel(*refs):
    arrays, out = refs[:-1], refs[-1]
    for slot in range(out.shape[0]):
        out[slot] = total_of(arrays, slot)


def prepare_kernel(moment, left, right, rot_old, left_plain, left_turned, right_tall, right_turned):
    for slot in range(rot_old.shape[0]):
        left_t, right_t = left[slot].T, right[slot].T
        half = product(as_left(moment[slot]), as_right(right[slot]))
        left_turned[slot] = as_left(left_t)
        rot_old[slot] = product(as_left(left_t), as_right(half))
        left_plain[slot] = as_left(left[slot])
        right_tall[slot] = as_left(right[slot], 0)
        right_turned[slot] = as_right(right_t)


def rotate(gradient, rot_old, second, left_turned, right_tall, right_turned, c, pairs):
    halves = [dot(jnp.concatenate([gradient[i]] * 2, 1), right_tall[slot], NN) for i, slot in pairs]
    rotated = [
        product(left_turned[slot], as_right(half)) for half, (_, slot) in zip(halves, pairs, strict=True)
    ]
    turned = []
    for value, (_, slot) in zip(rotated, pairs, strict=True):
        rot_moment = 0.95 * rot_old[slot] + 0.05 * value
        second_new = 0.95 * second[slot] + 0.05 * value * value
        scaled = rot_moment / c / (jnp.sqrt(second_new / c) + 1e-08)
        turned.append(product(as_left(scaled), right_turned[slot]))
    return turned


def step_kernel(grid, table, info, correction, *refs):
    parts = refs[: table.shares]
    (rot_old, second, master, left_plain, left_turned, right_tall, right_turned) = refs[table.shares : -2]
    gradient, updated = refs[-2:]
    rows = parts[0].shape[1]
    dp = info[table.place]
    group, share = lax.div(dp, table.shares), lax.rem(dp, table.shares)
    for dd in range(table.shares):
        gradient[:, pl.ds(pl.multiple_of((share ^ dd) * rows, rows), rows), :] = parts[dd][...]
    mine = pl.ds(pl.multiple_of(share * rows, rows), rows)
    pairs = [(index, table.slot(info, group, index)) for index in range(table.each)]
    turned = rotate(
        gradient, rot_old, second, left_turned, right_tall, right_turned, correction[0], pairs
    )
    for value, (index, slot) in zip(turned, pairs, strict=True):
        weights = master[slot, mine]
        moved = product(left_plain[slot, mine], as_right(value))
        moved = jnp.where(slot < info[table.held], moved, 0.0)
        updated[index] = (weights - 0.01 * (moved + 0.1 * weights)).astype(BF16)


def direction_kernel(table, info, correction, *refs):
    gradients = refs[: table.groups]
    (rot_old, second, left_plain, left_turned, right_tall, right_turned, direction) = refs[table.groups :]
    group = lax.div(info[table.place], table.shares)
    for dg, gradient in enumerate(gradients):
        pairs = [(index, table.slot(info, group ^ dg, index)) for index in range(table.each)]
        turned = rotate(
            gradient, rot_old, second, left_turned, right_tall, right_turned, correction[0], pairs
        )
        for value, (_, slot) in zip(turned, pairs, strict=True):
            moved = product(left_plain[slot], as_right(value))
            direction[slot] = jnp.where(slot < info[table.held], moved, 0.0)


def refresh(gradient, left_stat, right_stat, left, right, pairs):
    iterates = []
    for dims, stat, basis in ((NT, left_stat, left), (TN, right_stat, right)):
        for index, slot in pairs:
            gram = dot(gradient[index], gradient[index], dims)
            power = product(as_left(0.95 * stat[slot] + 0.05 * gram), as_right(basis[slot]))
            iterates.append(power / (jnp.sqrt(jnp.sum(power * power)) + 1e-06))
    for _ in range(NS_ITERS):
        squares = [product(as_left(x, 0), as_right(x), TN) for x in iterates]
        iterates = [
            1.5 * x - 0.5 * product(as_left(x), as_right(square))
            for x, square in zip(iterates, squares, strict=True)
        ]
    return iterates[: len(pairs)], iterates[len(pairs) :]


def refresh_kernel(table, first, info, *refs):
    count = table.groups - 1 if first else 1
    gradients, (left_stat, right_stat, left, right) = refs[:count], refs[count : count + 4]
    done, (left_out, right_out) = refs[count + 4 : -2], refs[-2:]
    group = lax.div(info[table.place], table.shares)

    def put(slot, new_left, new_right):
        live = slot < info[table.held]
        left_out[slot] = jnp.where(live, new_left, left[slot])
        right_out[slot] = jnp.where(live, new_right, right[slot])

    for dg, gradient in enumerate(gradients, first):
        pairs = [(index, table.slot(info, group ^ dg, index)) for index in range(table.each)]
        new_left, new_right = refresh(gradient, left_stat, right_stat, left, right, pairs)
        for index, slot in pairs:
            if first:
                put(slot, new_left[index], new_right[index])
            else:
                left_out[index], right_out[index] = new_left[index], new_right[index]
    if first:
        for index in range(table.each):
            put(table.slot(info, group, index), done[0][index], done[1][index])


def join_kernel(grid, table, info, *refs):
    arrays, (out, every) = refs[: grid.high], refs[-2:]
    spare = info[table.counts + part_index(grid, table, info)]
    for dh in range(grid.high):
        first = table.inverse + (info[table.place + 1] ^ dh) * table.each
        for index in range(table.each):
            at = info[first + index]
            every[jnp.where(at < 0, spare, at)] = arrays[dh][index]
            spare = spare + (at < 0).astype(jnp.int32)
    out[...] = every[: out.shape[0]]


def part_index(grid, table, info):
    column = info[table.place + 2] * grid.core + info[table.place + 3]
    return column * table.groups + lax.div(info[table.place], table.shares)


def weights_kernel(grid, table, info, *refs):
    arrays, (out, sem) = refs[:-2], refs[-2:]
    rows = arrays[0].shape[1]
    sources = [(dc, dm, dd) for dc in range(grid.core) for dm in range(grid.middle) for dd in range(grid.dp)]
    for array, source in zip(arrays, sources, strict=True):
        count, first, share = part_of(grid, table, info, *source)
        part = pl.ds(pl.multiple_of(share * rows, rows), rows)

        def put(array, first, part, at, carry):
            pltpu.make_async_copy(array.at[at], out.at[info[first + at], part], sem).start()
            return carry

        lax.fori_loop(0, count, functools.partial(put, array, first, part), 0)
    pltpu.make_async_copy(out, out, sem).wait()


def body(
    partials,
    owners,
    step_count,
    master,
    moment,
    second,
    stat_left,
    stat_right,
    basis_left,
    basis_right,
):
    grid = Grid(lax.axis_size("dp"), lax.axis_size("owner"))
    table = Table(grid, master.shape[0])
    chain = Chain()
    correction = 1.0 - jnp.power(jnp.float32(0.95), step_count.astype(F32))
    own = partials[0]
    other = grid.swap(own, core=1)
    (fetched,) = chain.call(copy_kernel, (), (own,), [shape(own.shape, BF16)])
    info, level = chain.call(
        functools.partial(table_kernel, grid, table),
        (grid.place(), owners),
        (),
        [shape((table.size,), jnp.int32), shape((1,), jnp.int32)],
        scratch=(pltpu.SMEM((grid.owners,), jnp.int32),),
        specs=[SMEM, SMEM],
        moved=8 * 1024 * 1024,
    )
    states = (master, moment, second, stat_left, stat_right, basis_left, basis_right)
    return lax.switch(
        level[0],
        [functools.partial(update, grid, table, room) for room in table.rooms],
        chain.token,
        info,
        fetched,
        other,
        correction,
        *states,
    )


def update(
    grid,
    table,
    room,
    token,
    info,
    own,
    other,
    correction,
    master,
    moment,
    second,
    stat_left,
    stat_right,
    basis_left,
    basis_right,
):
    slots, size = master.shape[:2]
    blocks = own.shape[0]
    rows = size // table.shares
    chain = Chain()
    chain.token = token
    share = shape((table.each, rows, size), BF16)
    main = shape((room, rows, size), BF16)
    group_state = shape((table.each, size, size), F32)
    group_gradient = shape((table.each, size, size), BF16)
    state = shape((slots, size, size), F32)
    plane = [(dm, dd) for dm in range(grid.middle) for dd in range(grid.dp)]
    passes = slots * size**3

    def over_plane(arrays):
        order = sorted(range(1, len(plane)), key=lambda index: plane[index], reverse=True)
        got = {index: grid.swap(arrays[index], middle=plane[index][0], dp=plane[index][1]) for index in order}
        return [arrays[0]] + [got[index] for index in range(1, len(plane))]

    def over_high(arrays):
        return [arrays[0]] + [grid.swap(arrays[dh], high=dh) for dh in range(1, grid.high)]

    outs = chain.call(
        functools.partial(spread_kernel, grid, table), (info,), (own, other), [main] * len(plane)
    )
    got = over_plane(outs)
    rot_old, left_plain, left_turned, right_tall, right_turned = chain.call(
        prepare_kernel,
        (),
        (moment, basis_left, basis_right),
        [
            state,
            shape((slots, size, 2 * size), BF16),
            shape((slots, size, 2 * size), BF16),
            shape((slots, 2 * size, size), BF16),
            shape((slots, 2 * size, 2 * size), BF16),
        ],
        16 * passes,
    )
    outs = chain.call(
        functools.partial(gather_sum_kernel, grid, table), (info,), got, [share] * grid.high
    )
    (summed,) = chain.call(sum_kernel, (), over_high(outs), [share])
    parts = [summed] + [grid.swap(summed, dp=dd) for dd in range(1, table.shares)]
    gradient, updated = chain.call(
        functools.partial(step_kernel, grid, table),
        (info, correction),
        (*parts, rot_old, second, master, left_plain, left_turned, right_tall, right_turned),
        [group_gradient, share],
        14 * passes,
    )
    spread = over_high([updated] * grid.high)
    others = [grid.swap(gradient, dp=dg * table.shares) for dg in range(1, table.groups)]
    done = chain.call(
        functools.partial(refresh_kernel, table, 0),
        (info,),
        (gradient, stat_left, stat_right, basis_left, basis_right),
        [group_state, group_state],
        100 * passes,
    )
    (joined,) = chain.call(
        functools.partial(join_kernel, grid, table),
        (info,),
        (*spread, *others),
        [main],
        scratch=(pltpu.VMEM((table.length, rows, size), BF16),),
    )
    got = over_plane([joined] * len(plane))
    (direction,) = chain.call(
        functools.partial(direction_kernel, table),
        (info, correction),
        (gradient, *others, rot_old, second, left_plain, left_turned, right_tall, right_turned),
        [state],
        36 * passes,
    )
    left_new, right_new = chain.call(
        functools.partial(refresh_kernel, table, 1),
        (info,),
        (*others, stat_left, stat_right, basis_left, basis_right, *done),
        [state, state],
        100 * passes,
    )
    (got[-1],) = chain.call(copy_kernel, (), (got[-1],), [main])
    (weights_all,) = chain.call(
        functools.partial(weights_kernel, grid, table),
        (info,),
        (*got, *(grid.swap(a, core=1) for a in got)),
        [shape((blocks, size, size), BF16)],
        scratch=(pltpu.SemaphoreType.DMA,),
        specs=[HBM],
    )
    return (weights_all, direction, left_new, right_new)


def solution(mesh):
    placed = (
        P(("dp", "owner"), None, None, None),
        P(),
        P(),
        P("owner", None, None),
        P("owner", None, None),
        P("owner", None, None),
        P("owner", None, None),
        P("owner", None, None),
        P("owner", None, None),
        P("owner", None, None),
    )
    return jax.shard_map(
        body,
        mesh=mesh,
        in_specs=placed,
        out_specs=(P(), P("owner", None, None), P("owner", None, None), P("owner", None, None)),
        check_vma=False,
    )
```

```python
import functools
import math

import jax
import jax.numpy as jnp
from jax import lax
from jax.experimental import pallas as pl
from jax.experimental.pallas import tpu as pltpu
from jax.sharding import PartitionSpec as P

NS_ITERS = 6
AXES = ("dp", "owner")
F32 = jnp.float32
BF16 = jnp.bfloat16
VMEM_LIMIT = 48 * 1024 * 1024
VMEM = pl.BlockSpec(memory_space=pltpu.VMEM)
SMEM = pl.BlockSpec(memory_space=pltpu.SMEM)
HBM = pl.BlockSpec(memory_space=pltpu.HBM)


def shape(dims, dtype):
    return jax.ShapeDtypeStruct(dims, dtype)


class Chain:
    def __init__(self):
        self.token = None

    def call(self, kernel, scalars, arrays, outs, flops=0, scratch=(), specs=None, moved=0, reuse=None):
        moved = moved or sum(math.prod(a.shape) * a.dtype.itemsize for a in [*arrays, *outs])
        count = len(scalars) + len(arrays)
        tokens = () if self.token is None else (self.token,)
        kept = () if reuse is None else (reuse,)
        count_in = count + len(tokens) + len(kept)
        specs = specs or [VMEM] * len(outs)

        def run(*refs):
            refs = list(refs)
            token = refs.pop(count_in + len(outs))
            kernel(*refs[:count], *refs[count_in:])
            token[...] = jnp.zeros_like(token)

        *results, self.token = pl.pallas_call(
            run,
            out_shape=(*outs, shape((8, 128), F32)),
            in_specs=[SMEM] * len(scalars)
            + [VMEM] * len(arrays)
            + [VMEM] * len(tokens)
            + [HBM] * len(kept),
            out_specs=(*specs, VMEM),
            scratch_shapes=list(scratch),
            input_output_aliases={count_in - 1: 0} if kept else {},
            compiler_params=pltpu.CompilerParams(vmem_limit_bytes=VMEM_LIMIT),
            cost_estimate=pl.CostEstimate(flops=flops, bytes_accessed=moved, transcendentals=0),
        )(*(pltpu.with_memory_space_constraint(a, pltpu.SMEM) for a in scalars), *arrays, *tokens, *kept)
        return results


class Grid:
    def __init__(self, dp_count, owner_count):
        self.dp, self.core = dp_count, 2
        self.high = 4
        self.middle = owner_count // (self.core * self.high)
        self.owners = owner_count

    def place(self):
        owner = lax.axis_index("owner")
        high, rest = lax.div(owner, self.core * self.middle), lax.rem(owner, self.core * self.middle)
        return lax.axis_index("dp"), high, lax.div(rest, self.core), lax.rem(rest, self.core)

    def swap(self, array, dp=0, high=0, middle=0, core=0):
        step = (high * self.middle + middle) * self.core + core
        pairs = [
            (d * self.owners + o, (d ^ dp) * self.owners + (o ^ step))
            for d in range(self.dp)
            for o in range(self.owners)
        ]
        return lax.ppermute(array, AXES, pairs)


def split(value):
    top = value.astype(BF16)
    return top, (value - top.astype(F32)).astype(BF16)


def dot(left, right, dims):
    return lax.dot_general(left, right, (dims, ((), ())), preferred_element_type=F32)


NN = ((1,), (0,))
NT = ((1,), (1,))
TN = ((0,), (0,))


def as_left(value, axis=1):
    return jnp.concatenate(split(value), axis)


def as_right(value):
    half = jnp.concatenate(split(value), 1)
    return jnp.concatenate([half, half], 0)


def product(left, right, dims=NN):
    wide = dot(left, right, dims)
    size = wide.shape[1] // 2
    return wide[:, :size] + wide[:, size:]


def log2(count):
    return count.bit_length() - 1


class Table:
    def __init__(self, grid, slots):
        self.columns = grid.middle * grid.core
        self.groups = math.gcd(slots, grid.dp)
        self.shares = grid.dp // self.groups
        self.each = slots // self.groups
        self.length = grid.high * self.each
        self.rooms = (self.length * 2 // 3, self.length * 3 // 4, self.length)
        self.listed = 0
        self.counts = self.columns * self.groups * self.length
        self.inverse = self.counts + self.columns * self.groups
        self.held = self.inverse + self.length
        self.place = self.held + 1
        self.size = self.place + 4

    def slot(self, info, group, index):
        turn = group + self.groups - lax.rem(info[self.place + 1], self.groups)
        return self.groups * index + lax.rem(turn, self.groups)


def table_kernel(grid, table, owners, source, out, level, fetched, seen, sem):
    copy = pltpu.make_async_copy(source, fetched, sem)
    copy.start()
    place = grid.place()
    for owner in range(grid.owners):
        seen[owner] = 0
    for part in range(table.columns * table.groups):
        out[table.counts + part] = 0
    for at in range(table.length):
        out[table.inverse + at] = -1
    column_mine = place[2] * grid.core + place[3]
    mine = column_mine * table.groups + lax.div(place[0], table.shares)

    def step(block, carry):
        owner = owners[block]
        rank = seen[owner]
        seen[owner] = rank + 1
        column, high = owner & (table.columns - 1), owner >> log2(table.columns)
        group, index = (rank + high) & (table.groups - 1), rank >> log2(table.groups)
        part = column * table.groups + group
        at = out[table.counts + part]
        out[table.counts + part] = at + 1
        out[table.listed + part * table.length + at] = block

        @pl.when(part == mine)
        def _():
            out[table.inverse + high * table.each + index] = at

        return carry

    lax.fori_loop(0, owners.shape[0], step, 0, unroll=8)
    out[table.held] = seen[place[1] * table.columns + column_mine]
    most = out[table.counts]
    for part in range(1, table.columns * table.groups):
        most = jnp.maximum(most, out[table.counts + part])
    level[0] = sum((most > room).astype(jnp.int32) for room in table.rooms[:-1])
    for at in range(4):
        out[table.place + at] = place[at]
    copy.wait()


def part_of(grid, table, info, dc, dm, dd):
    column = (info[table.place + 2] ^ dm) * grid.core + (info[table.place + 3] ^ dc)
    dp = info[table.place] ^ dd
    part = column * table.groups + lax.div(dp, table.shares)
    return info[table.counts + part], table.listed + part * table.length, lax.rem(dp, table.shares)


def copy_kernel(source, out):
    out[...] = source[...]


def spread_kernel(grid, table, info, own, other, *outs):
    rows = own.shape[1] // table.shares
    for dm in range(grid.middle):
        for dd in range(grid.dp):
            count, first, share = part_of(grid, table, info, 0, dm, dd)
            part = pl.ds(pl.multiple_of(share * rows, rows), rows)

            def put(out, at, carry):
                block = info[first + at]
                total = own[block, part].astype(F32) + other[block, part].astype(F32)
                out[at] = total.astype(BF16)
                return carry

            lax.fori_loop(0, count, functools.partial(put, outs[dm * grid.dp + dd]), 0)


def total_of(arrays, at):
    total = arrays[0][at].astype(F32)
    for array in arrays[1:]:
        total = total + array[at].astype(F32)
    return total.astype(BF16)


def gather_sum_kernel(grid, table, info, *refs):
    count = grid.middle * grid.dp
    arrays, outs = refs[:count], refs[count:]
    for dh in range(grid.high):
        first = table.inverse + (info[table.place + 1] ^ dh) * table.each
        for index in range(table.each):
            at = jnp.clip(info[first + index], 0, arrays[0].shape[0] - 1)
            outs[dh][index] = total_of(arrays, at)


def sum_kernel(*refs):
    arrays, out = refs[:-1], refs[-1]
    for slot in range(out.shape[0]):
        out[slot] = total_of(arrays, slot)


def prepare_kernel(moment, left, right, rot_old, left_plain, left_turned, right_tall, right_turned):
    for slot in range(rot_old.shape[0]):
        left_t, right_t = left[slot].T, right[slot].T
        half = product(as_left(moment[slot]), as_right(right[slot]))
        left_turned[slot] = as_left(left_t)
        rot_old[slot] = product(as_left(left_t), as_right(half))
        left_plain[slot] = as_left(left[slot])
        right_tall[slot] = as_left(right[slot], 0)
        right_turned[slot] = as_right(right_t)


def rotate(gradient, rot_old, second, left_turned, right_tall, right_turned, c, pairs):
    halves = [dot(jnp.concatenate([gradient[i]] * 2, 1), right_tall[slot], NN) for i, slot in pairs]
    rotated = [
        product(left_turned[slot], as_right(half)) for half, (_, slot) in zip(halves, pairs, strict=True)
    ]
    turned = []
    for value, (_, slot) in zip(rotated, pairs, strict=True):
        rot_moment = 0.95 * rot_old[slot] + 0.05 * value
        second_new = 0.95 * second[slot] + 0.05 * value * value
        scaled = rot_moment / c / (jnp.sqrt(second_new / c) + 1e-08)
        turned.append(product(as_left(scaled), right_turned[slot]))
    return turned


def step_kernel(grid, table, info, correction, *refs):
    parts = refs[: table.shares]
    (rot_old, second, master, left_plain, left_turned, right_tall, right_turned) = refs[table.shares : -2]
    gradient, updated = refs[-2:]
    rows = parts[0].shape[1]
    dp = info[table.place]
    group, share = lax.div(dp, table.shares), lax.rem(dp, table.shares)
    for dd in range(table.shares):
        gradient[:, pl.ds(pl.multiple_of((share ^ dd) * rows, rows), rows), :] = parts[dd][...]
    mine = pl.ds(pl.multiple_of(share * rows, rows), rows)
    pairs = [(index, table.slot(info, group, index)) for index in range(table.each)]
    turned = rotate(
        gradient, rot_old, second, left_turned, right_tall, right_turned, correction[0], pairs
    )
    for value, (index, slot) in zip(turned, pairs, strict=True):
        weights = master[slot, mine]
        moved = product(left_plain[slot, mine], as_right(value))
        moved = jnp.where(slot < info[table.held], moved, 0.0)
        updated[index] = (weights - 0.01 * (moved + 0.1 * weights)).astype(BF16)


def direction_kernel(table, info, correction, *refs):
    gradients = refs[: table.groups]
    (rot_old, second, left_plain, left_turned, right_tall, right_turned, direction) = refs[table.groups :]
    group = lax.div(info[table.place], table.shares)
    for dg, gradient in enumerate(gradients):
        pairs = [(index, table.slot(info, group ^ dg, index)) for index in range(table.each)]
        turned = rotate(
            gradient, rot_old, second, left_turned, right_tall, right_turned, correction[0], pairs
        )
        for value, (_, slot) in zip(turned, pairs, strict=True):
            moved = product(left_plain[slot], as_right(value))
            direction[slot] = jnp.where(slot < info[table.held], moved, 0.0)


def refresh(gradient, left_stat, right_stat, left, right, pairs):
    iterates = []
    for dims, stat, basis in ((NT, left_stat, left), (TN, right_stat, right)):
        for index, slot in pairs:
            gram = dot(gradient[index], gradient[index], dims)
            power = product(as_left(0.95 * stat[slot] + 0.05 * gram), as_right(basis[slot]))
            iterates.append(power / (jnp.sqrt(jnp.sum(power * power)) + 1e-06))
    for _ in range(NS_ITERS):
        squares = [product(as_left(x, 0), as_right(x), TN) for x in iterates]
        iterates = [
            1.5 * x - 0.5 * product(as_left(x), as_right(square))
            for x, square in zip(iterates, squares, strict=True)
        ]
    return iterates[: len(pairs)], iterates[len(pairs) :]


def refresh_kernel(table, first, info, *refs):
    count = table.groups - 1 if first else 1
    gradients, (left_stat, right_stat, left, right) = refs[:count], refs[count : count + 4]
    done, (left_out, right_out) = refs[count + 4 : -2], refs[-2:]
    group = lax.div(info[table.place], table.shares)

    def put(slot, new_left, new_right):
        live = slot < info[table.held]
        left_out[slot] = jnp.where(live, new_left, left[slot])
        right_out[slot] = jnp.where(live, new_right, right[slot])

    for dg, gradient in enumerate(gradients, first):
        pairs = [(index, table.slot(info, group ^ dg, index)) for index in range(table.each)]
        new_left, new_right = refresh(gradient, left_stat, right_stat, left, right, pairs)
        for index, slot in pairs:
            if first:
                put(slot, new_left[index], new_right[index])
            else:
                left_out[index], right_out[index] = new_left[index], new_right[index]
    if first:
        for index in range(table.each):
            put(table.slot(info, group, index), done[0][index], done[1][index])


def join_kernel(grid, table, info, *refs):
    arrays, (out, every) = refs[: grid.high], refs[-2:]
    spare = info[table.counts + part_index(grid, table, info)]
    for dh in range(grid.high):
        first = table.inverse + (info[table.place + 1] ^ dh) * table.each
        for index in range(table.each):
            at = info[first + index]
            every[jnp.where(at < 0, spare, at)] = arrays[dh][index]
            spare = spare + (at < 0).astype(jnp.int32)
    out[...] = every[: out.shape[0]]


def part_index(grid, table, info):
    column = info[table.place + 2] * grid.core + info[table.place + 3]
    return column * table.groups + lax.div(info[table.place], table.shares)


def weights_kernel(grid, table, core, info, *refs):
    arrays, (out, sem) = refs[: grid.middle * grid.dp], refs[-2:]
    rows = arrays[0].shape[1]

    def each(act):
        for index, array in enumerate(arrays):
            count, first, share = part_of(grid, table, info, core, index // grid.dp, index % grid.dp)
            part = pl.ds(pl.multiple_of(share * rows, rows), rows)

            def put(at, carry):
                act(pltpu.make_async_copy(array.at[at], out.at[info[first + at], part], sem))
                return carry

            lax.fori_loop(0, count, put, 0)

    each(lambda copy: copy.start())
    each(lambda copy: copy.wait())


def body(
    partials,
    owners,
    step_count,
    master,
    moment,
    second,
    stat_left,
    stat_right,
    basis_left,
    basis_right,
):
    grid = Grid(lax.axis_size("dp"), lax.axis_size("owner"))
    table = Table(grid, master.shape[0])
    own = partials[0]
    other = grid.swap(own, core=1)
    info, level, fetched = pl.pallas_call(
        functools.partial(table_kernel, grid, table),
        out_shape=(
            pltpu.SMEM((table.size,), jnp.int32),
            pltpu.SMEM((1,), jnp.int32),
            pltpu.VMEM(own.shape, BF16),
        ),
        in_specs=[SMEM, HBM],
        out_specs=(SMEM, SMEM, VMEM),
        scratch_shapes=[pltpu.SMEM((grid.owners,), jnp.int32), pltpu.SemaphoreType.DMA],
        compiler_params=pltpu.CompilerParams(vmem_limit_bytes=VMEM_LIMIT),
    )(
        pltpu.with_memory_space_constraint(owners, pltpu.SMEM),
        pltpu.with_memory_space_constraint(own, pltpu.HBM),
    )
    states = (master, moment, second, stat_left, stat_right, basis_left, basis_right)
    return lax.switch(
        level[0],
        [functools.partial(update, grid, table, room) for room in table.rooms],
        info,
        fetched,
        other,
        step_count,
        *states,
    )


def update(
    grid,
    table,
    room,
    info,
    own,
    other,
    step_count,
    master,
    moment,
    second,
    stat_left,
    stat_right,
    basis_left,
    basis_right,
):
    slots, size = master.shape[:2]
    blocks = own.shape[0]
    rows = size // table.shares
    chain = Chain()
    correction = 1.0 - jnp.power(jnp.float32(0.95), step_count.astype(F32))
    share = shape((table.each, rows, size), BF16)
    main = shape((room, rows, size), BF16)
    group_state = shape((table.each, size, size), F32)
    group_gradient = shape((table.each, size, size), BF16)
    state = shape((slots, size, size), F32)
    plane = [(dm, dd) for dm in range(grid.middle) for dd in range(grid.dp)]
    passes = slots * size**3

    def over_plane(arrays):
        order = sorted(range(1, len(plane)), key=lambda index: plane[index], reverse=True)
        got = {index: grid.swap(arrays[index], middle=plane[index][0], dp=plane[index][1]) for index in order}
        return [arrays[0]] + [got[index] for index in range(1, len(plane))]

    def over_high(arrays):
        return [arrays[0]] + [grid.swap(arrays[dh], high=dh) for dh in range(1, grid.high)]

    outs = chain.call(
        functools.partial(spread_kernel, grid, table), (info,), (own, other), [main] * len(plane)
    )
    got = over_plane(outs)
    rot_old, left_plain, left_turned, right_tall, right_turned = chain.call(
        prepare_kernel,
        (),
        (moment, basis_left, basis_right),
        [
            state,
            shape((slots, size, 2 * size), BF16),
            shape((slots, size, 2 * size), BF16),
            shape((slots, 2 * size, size), BF16),
            shape((slots, 2 * size, 2 * size), BF16),
        ],
        16 * passes,
    )
    outs = chain.call(
        functools.partial(gather_sum_kernel, grid, table), (info,), got, [share] * grid.high
    )
    (summed,) = chain.call(sum_kernel, (), over_high(outs), [share])
    parts = [summed] + [grid.swap(summed, dp=dd) for dd in range(1, table.shares)]
    gradient, updated = chain.call(
        functools.partial(step_kernel, grid, table),
        (info, correction),
        (*parts, rot_old, second, master, left_plain, left_turned, right_tall, right_turned),
        [group_gradient, share],
        14 * passes,
    )
    spread = over_high([updated] * grid.high)
    others = [grid.swap(gradient, dp=dg * table.shares) for dg in range(1, table.groups)]
    done = chain.call(
        functools.partial(refresh_kernel, table, 0),
        (info,),
        (gradient, stat_left, stat_right, basis_left, basis_right),
        [group_state, group_state],
        100 * passes,
    )
    (joined,) = chain.call(
        functools.partial(join_kernel, grid, table),
        (info,),
        (*spread, *others),
        [main],
        scratch=(pltpu.VMEM((table.length, rows, size), BF16),),
    )
    got = over_plane([joined] * len(plane))
    (direction,) = chain.call(
        functools.partial(direction_kernel, table),
        (info, correction),
        (gradient, *others, rot_old, second, left_plain, left_turned, right_tall, right_turned),
        [state],
        36 * passes,
    )
    left_new, right_new = chain.call(
        functools.partial(refresh_kernel, table, 1),
        (info,),
        (*others, stat_left, stat_right, basis_left, basis_right, *done),
        [state, state],
        100 * passes,
    )
    (got[-1],) = chain.call(copy_kernel, (), (got[-1],), [main])
    weights_all = pltpu.HBM((blocks, size, size), BF16)
    (weights_own,) = chain.call(
        functools.partial(weights_kernel, grid, table, 0),
        (info,),
        got,
        [weights_all],
        scratch=(pltpu.SemaphoreType.DMA,),
        specs=[HBM],
    )
    (weights_all,) = chain.call(
        functools.partial(weights_kernel, grid, table, 1),
        (info,),
        [grid.swap(a, core=1) for a in got],
        [weights_all],
        scratch=(pltpu.SemaphoreType.DMA,),
        specs=[HBM],
        reuse=weights_own,
    )
    return (weights_all, direction, left_new, right_new)


def solution(mesh):
    placed = (
        P(("dp", "owner"), None, None, None),
        P(),
        P(),
        P("owner", None, None),
        P("owner", None, None),
        P("owner", None, None),
        P("owner", None, None),
        P("owner", None, None),
        P("owner", None, None),
        P("owner", None, None),
    )
    return jax.shard_map(
        body,
        mesh=mesh,
        in_specs=placed,
        out_specs=(P(), P("owner", None, None), P("owner", None, None), P("owner", None, None)),
        check_vma=False,
    )
```

```python
import functools
import math

import jax
import jax.numpy as jnp
from jax import lax
from jax.experimental import pallas as pl
from jax.experimental.pallas import tpu as pltpu
from jax.sharding import PartitionSpec as P

NS_ITERS = 6
AXES = ("dp", "owner")
F32 = jnp.float32
BF16 = jnp.bfloat16
VMEM_LIMIT = 48 * 1024 * 1024
VMEM = pl.BlockSpec(memory_space=pltpu.VMEM)
SMEM = pl.BlockSpec(memory_space=pltpu.SMEM)
HBM = pl.BlockSpec(memory_space=pltpu.HBM)


def shape(dims, dtype):
    return jax.ShapeDtypeStruct(dims, dtype)


class Chain:
    def __init__(self):
        self.token = None

    def call(self, kernel, scalars, arrays, outs, flops=0, scratch=(), specs=None, moved=0, reuse=()):
        moved = moved or sum(math.prod(a.shape) * a.dtype.itemsize for a in [*arrays, *outs])
        count = len(scalars) + len(arrays)
        tokens = () if self.token is None else (self.token,)
        kept = count + len(tokens)
        count_in = kept + len(reuse)
        specs = specs or [VMEM] * len(outs)

        def run(*refs):
            refs = list(refs)
            token = refs.pop(count_in + len(outs))
            kernel(*refs[:count], *refs[count_in:])
            token[...] = jnp.zeros_like(token)

        *results, self.token = pl.pallas_call(
            run,
            out_shape=(*outs, shape((8, 128), F32)),
            in_specs=[SMEM] * len(scalars)
            + [VMEM] * len(arrays)
            + [VMEM] * len(tokens)
            + [HBM] * len(reuse),
            out_specs=(*specs, VMEM),
            scratch_shapes=list(scratch),
            input_output_aliases={kept + index: index for index in range(len(reuse))},
            compiler_params=pltpu.CompilerParams(vmem_limit_bytes=VMEM_LIMIT),
            cost_estimate=pl.CostEstimate(flops=flops, bytes_accessed=moved, transcendentals=0),
        )(*(pltpu.with_memory_space_constraint(a, pltpu.SMEM) for a in scalars), *arrays, *tokens, *reuse)
        return results


class Grid:
    def __init__(self, dp_count, owner_count):
        self.dp, self.core = dp_count, 2
        self.high = 4
        self.middle = owner_count // (self.core * self.high)
        self.owners = owner_count

    def place(self):
        owner = lax.axis_index("owner")
        high, rest = lax.div(owner, self.core * self.middle), lax.rem(owner, self.core * self.middle)
        return lax.axis_index("dp"), high, lax.div(rest, self.core), lax.rem(rest, self.core)

    def swap(self, array, dp=0, high=0, middle=0, core=0):
        step = (high * self.middle + middle) * self.core + core
        pairs = [
            (d * self.owners + o, (d ^ dp) * self.owners + (o ^ step))
            for d in range(self.dp)
            for o in range(self.owners)
        ]
        return lax.ppermute(array, AXES, pairs)


def split(value):
    top = value.astype(BF16)
    return top, (value - top.astype(F32)).astype(BF16)


def dot(left, right, dims):
    return lax.dot_general(left, right, (dims, ((), ())), preferred_element_type=F32)


NN = ((1,), (0,))
NT = ((1,), (1,))
TN = ((0,), (0,))


def as_left(value, axis=1):
    return jnp.concatenate(split(value), axis)


def as_right(value):
    half = jnp.concatenate(split(value), 1)
    return jnp.concatenate([half, half], 0)


def product(left, right, dims=NN):
    wide = dot(left, right, dims)
    size = wide.shape[1] // 2
    return wide[:, :size] + wide[:, size:]


def log2(count):
    return count.bit_length() - 1


class Table:
    def __init__(self, grid, slots):
        self.columns = grid.middle * grid.core
        self.groups = math.gcd(slots, grid.dp)
        self.shares = grid.dp // self.groups
        self.each = slots // self.groups
        self.length = grid.high * self.each
        self.rooms = (self.length * 2 // 3, self.length * 3 // 4, self.length)
        self.listed = 0
        self.counts = self.columns * self.groups * self.length
        self.inverse = self.counts + self.columns * self.groups
        self.held = self.inverse + self.length
        self.place = self.held + 1
        self.size = self.place + 4

    def slot(self, info, group, index):
        turn = group + self.groups - lax.rem(info[self.place + 1], self.groups)
        return self.groups * index + lax.rem(turn, self.groups)


def table_kernel(grid, table, owners, source, out, level, fetched, seen, sem):
    copy = pltpu.make_async_copy(source, fetched, sem)
    copy.start()
    place = grid.place()
    for owner in range(grid.owners):
        seen[owner] = 0
    for part in range(table.columns * table.groups):
        out[table.counts + part] = 0
    for at in range(table.length):
        out[table.inverse + at] = -1
    column_mine = place[2] * grid.core + place[3]
    mine = column_mine * table.groups + lax.div(place[0], table.shares)

    def step(block, carry):
        owner = owners[block]
        rank = seen[owner]
        seen[owner] = rank + 1
        column, high = owner & (table.columns - 1), owner >> log2(table.columns)
        group, index = (rank + high) & (table.groups - 1), rank >> log2(table.groups)
        part = column * table.groups + group
        at = out[table.counts + part]
        out[table.counts + part] = at + 1
        out[table.listed + part * table.length + at] = block

        @pl.when(part == mine)
        def _():
            out[table.inverse + high * table.each + index] = at

        return carry

    lax.fori_loop(0, owners.shape[0], step, 0, unroll=8)
    out[table.held] = seen[place[1] * table.columns + column_mine]
    most = out[table.counts]
    for part in range(1, table.columns * table.groups):
        most = jnp.maximum(most, out[table.counts + part])
    level[0] = sum((most > room).astype(jnp.int32) for room in table.rooms[:-1])
    for at in range(4):
        out[table.place + at] = place[at]
    copy.wait()


def part_of(grid, table, info, dc, dm, dd):
    column = (info[table.place + 2] ^ dm) * grid.core + (info[table.place + 3] ^ dc)
    dp = info[table.place] ^ dd
    part = column * table.groups + lax.div(dp, table.shares)
    return info[table.counts + part], table.listed + part * table.length, lax.rem(dp, table.shares)


def copy_kernel(source, out):
    out[...] = source[...]


def spread_kernel(grid, table, cuts, info, own, other, *outs):
    rows = own.shape[1] // table.shares
    pieces = len(cuts) - 1
    for index in range(grid.middle * grid.dp):
        count, first, share = part_of(grid, table, info, 0, index // grid.dp, index % grid.dp)
        part = pl.ds(pl.multiple_of(share * rows, rows), rows)
        for piece in range(pieces):
            out = outs[index * pieces + piece]

            def put(at, carry):
                block = info[first + at]
                total = own[block, part].astype(F32) + other[block, part].astype(F32)
                out[at - cuts[piece]] = total.astype(BF16)
                return carry

            lax.fori_loop(cuts[piece], jnp.minimum(count, cuts[piece + 1]), put, 0)


def total_of(arrays, at):
    total = arrays[0][at].astype(F32)
    for array in arrays[1:]:
        total = total + array[at].astype(F32)
    return total.astype(BF16)


def gather_sum_kernel(grid, table, cuts, info, *refs):
    arrays, outs, every = refs[: -1 - grid.high], refs[-1 - grid.high : -1], refs[-1]
    each = len(arrays) // (len(cuts) - 1)
    for piece, (begin, end) in enumerate(zip(cuts, cuts[1:])):
        for at in range(begin, end):
            every[at] = total_of(arrays[piece * each : (piece + 1) * each], at - begin)
    for dh in range(grid.high):
        first = table.inverse + (info[table.place + 1] ^ dh) * table.each
        for index in range(table.each):
            outs[dh][index] = every[jnp.clip(info[first + index], 0, cuts[-1] - 1)]


def merge_kernel(*refs):
    count = len(refs) // 3
    for one, two, out in zip(refs[:count], refs[count : 2 * count], refs[2 * count :], strict=True):
        for at in range(out.shape[0]):
            out[at] = total_of((one, two), at)


def sum_kernel(*refs):
    arrays, out = refs[:-1], refs[-1]
    for slot in range(out.shape[0]):
        out[slot] = total_of(arrays, slot)


def prepare_kernel(moment, left, right, rot_old, left_plain, left_turned, right_tall, right_turned):
    for slot in range(rot_old.shape[0]):
        left_t, right_t = left[slot].T, right[slot].T
        half = product(as_left(moment[slot]), as_right(right[slot]))
        left_turned[slot] = as_left(left_t)
        rot_old[slot] = product(as_left(left_t), as_right(half))
        left_plain[slot] = as_left(left[slot])
        right_tall[slot] = as_left(right[slot], 0)
        right_turned[slot] = as_right(right_t)


def rotate(gradient, rot_old, second, left_turned, right_tall, right_turned, c, pairs):
    halves = [dot(jnp.concatenate([gradient[i]] * 2, 1), right_tall[slot], NN) for i, slot in pairs]
    rotated = [
        product(left_turned[slot], as_right(half)) for half, (_, slot) in zip(halves, pairs, strict=True)
    ]
    turned = []
    for value, (_, slot) in zip(rotated, pairs, strict=True):
        rot_moment = 0.95 * rot_old[slot] + 0.05 * value
        second_new = 0.95 * second[slot] + 0.05 * value * value
        scaled = rot_moment / c / (jnp.sqrt(second_new / c) + 1e-08)
        turned.append(product(as_left(scaled), right_turned[slot]))
    return turned


def step_kernel(grid, table, info, correction, *refs):
    parts = refs[: table.shares]
    (rot_old, second, master, left_plain, left_turned, right_tall, right_turned) = refs[table.shares : -3]
    gradient, turned, updated = refs[-3:]
    rows = parts[0].shape[1]
    dp = info[table.place]
    group, share = lax.div(dp, table.shares), lax.rem(dp, table.shares)
    for dd in range(table.shares):
        gradient[:, pl.ds(pl.multiple_of((share ^ dd) * rows, rows), rows), :] = parts[dd][...]
    mine = pl.ds(pl.multiple_of(share * rows, rows), rows)
    pairs = [(index, table.slot(info, group, index)) for index in range(table.each)]
    values = rotate(
        gradient, rot_old, second, left_turned, right_tall, right_turned, correction[0], pairs
    )
    for value, (index, slot) in zip(values, pairs, strict=True):
        turned[index] = value
        weights = master[slot, mine]
        moved = product(left_plain[slot, mine], as_right(value))
        moved = jnp.where(slot < info[table.held], moved, 0.0)
        updated[index] = (weights - 0.01 * (moved + 0.1 * weights)).astype(BF16)


def refresh(gradient, left_stat, right_stat, left, right, pairs):
    iterates = []
    for dims, stat, basis in ((NT, left_stat, left), (TN, right_stat, right)):
        for index, slot in pairs:
            gram = dot(gradient[index], gradient[index], dims)
            power = product(as_left(0.95 * stat[slot] + 0.05 * gram), as_right(basis[slot]))
            iterates.append(power / (jnp.sqrt(jnp.sum(power * power)) + 1e-06))
    for _ in range(NS_ITERS):
        squares = [product(as_left(x, 0), as_right(x), TN) for x in iterates]
        iterates = [
            1.5 * x - 0.5 * product(as_left(x), as_right(square))
            for x, square in zip(iterates, squares, strict=True)
        ]
    return iterates[: len(pairs)], iterates[len(pairs) :]


def own_kernel(table, info, gradient, turned, left_plain, stat_left, stat_right, left, right, *refs):
    outs, (held, sem) = refs[:3], refs[3:]
    group = lax.div(info[table.place], table.shares)
    pairs = [(index, table.slot(info, group, index)) for index in range(table.each)]
    new_left, new_right = refresh(gradient, stat_left, stat_right, left, right, pairs)
    copies = []
    for index, slot in pairs:
        live = slot < info[table.held]
        moved = product(left_plain[slot], as_right(turned[index]))
        held[0, index] = jnp.where(live, moved, 0.0)
        held[1, index] = jnp.where(live, new_left[index], left[slot])
        held[2, index] = jnp.where(live, new_right[index], right[slot])
        copies += [pltpu.make_async_copy(held.at[n, index], outs[n].at[slot], sem) for n in range(3)]
    for copy in copies:
        copy.start()
    for copy in copies:
        copy.wait()


def others_kernel(table, info, *refs):
    count = table.groups - 1
    gradients, bases, (left_out, right_out) = refs[:count], refs[count : count + 4], refs[-2:]
    group = lax.div(info[table.place], table.shares)
    for dg, gradient in enumerate(gradients, 1):
        pairs = [(index, table.slot(info, group ^ dg, index)) for index in range(table.each)]
        new_left, new_right = refresh(gradient, *bases, pairs)
        for index, slot in pairs:
            at = (dg - 1) * table.each + index
            live = slot < info[table.held]
            left_out[at] = jnp.where(live, new_left[index], bases[2][slot])
            right_out[at] = jnp.where(live, new_right[index], bases[3][slot])


def finish_kernel(grid, table, layout, info, correction, *refs):
    count = table.groups - 1
    gradients, refs = refs[:count], refs[count:]
    (rot_old, second, left_plain, left_turned, right_tall, right_turned) = refs[:6]
    new_left, new_right, *packed = refs[6 : 8 + len(layout)]
    direction, left_out, right_out, weights, held, sem = refs[8 + len(layout) :]
    place_blocks(grid, table, layout, 0, info, packed, weights, sem, lambda copy: copy.start())
    group = lax.div(info[table.place], table.shares)
    every = [
        (dg, index, table.slot(info, group ^ dg, index))
        for dg in range(1, table.groups)
        for index in range(table.each)
    ]
    copies = []
    for at, (_, _, slot) in enumerate(every):
        copies.append(pltpu.make_async_copy(new_left.at[at], left_out.at[slot], sem))
        copies.append(pltpu.make_async_copy(new_right.at[at], right_out.at[slot], sem))
    for copy in copies:
        copy.start()
    for dg, gradient in enumerate(gradients, 1):
        pairs = [(index, slot) for owner, index, slot in every if owner == dg]
        turned = rotate(
            gradient, rot_old, second, left_turned, right_tall, right_turned, correction[0], pairs
        )
        for index, slot in pairs:
            moved = product(left_plain[slot], as_right(turned[index]))
            at = (dg - 1) * table.each + index
            held[at] = jnp.where(slot < info[table.held], moved, 0.0)
            copies.append(pltpu.make_async_copy(held.at[at], direction.at[slot], sem))
            copies[-1].start()
    for copy in copies:
        copy.wait()
    place_blocks(grid, table, layout, 0, info, packed, weights, sem, lambda copy: copy.wait())


def join_kernel(grid, table, cuts, info, *refs):
    pieces = len(cuts) - 1
    arrays, outs, every = refs[: grid.high], refs[-1 - pieces : -1], refs[-1]
    spare = info[table.counts + part_index(grid, table, info)]
    for dh in range(grid.high):
        first = table.inverse + (info[table.place + 1] ^ dh) * table.each
        for index in range(table.each):
            at = info[first + index]
            every[jnp.where(at < 0, spare, at)] = arrays[dh][index]
            spare = spare + (at < 0).astype(jnp.int32)
    for out, begin, end in zip(outs, cuts, cuts[1:]):
        out[...] = every[begin:end]


def pack_kernel(*refs):
    arrays, out = refs[:-1], refs[-1]
    begin = 0
    for array in arrays:
        out[begin : begin + array.shape[0]] = array[...]
        begin += array.shape[0]


def part_index(grid, table, info):
    column = info[table.place + 2] * grid.core + info[table.place + 3]
    return column * table.groups + lax.div(info[table.place], table.shares)


def place_blocks(grid, table, layout, core, info, packed, out, sem, act):
    rows = out.shape[1] // table.shares
    for array, pieces in zip(packed, layout, strict=True):
        base = 0
        for (dm, dd), begin, end in pieces:
            count, first, share = part_of(grid, table, info, core, dm, dd)
            part = pl.ds(pl.multiple_of(share * rows, rows), rows)

            def put(at, carry):
                source = array.at[base - begin + at]
                act(pltpu.make_async_copy(source, out.at[info[first + at], part], sem))
                return carry

            lax.fori_loop(begin, jnp.minimum(count, end), put, 0)
            base += end - begin


def weights_kernel(grid, table, layout, info, *refs):
    packed, (out, sem) = refs[:-2], refs[-2:]
    for act in (lambda copy: copy.start(), lambda copy: copy.wait()):
        place_blocks(grid, table, layout, 1, info, packed, out, sem, act)


def body(
    partials,
    owners,
    step_count,
    master,
    moment,
    second,
    stat_left,
    stat_right,
    basis_left,
    basis_right,
):
    grid = Grid(lax.axis_size("dp"), lax.axis_size("owner"))
    table = Table(grid, master.shape[0])
    own = partials[0]
    other = grid.swap(own, core=1)
    info, level, fetched = pl.pallas_call(
        functools.partial(table_kernel, grid, table),
        out_shape=(
            pltpu.SMEM((table.size,), jnp.int32),
            pltpu.SMEM((1,), jnp.int32),
            pltpu.VMEM(own.shape, BF16),
        ),
        in_specs=[SMEM, HBM],
        out_specs=(SMEM, SMEM, VMEM),
        scratch_shapes=[pltpu.SMEM((grid.owners,), jnp.int32), pltpu.SemaphoreType.DMA],
        compiler_params=pltpu.CompilerParams(vmem_limit_bytes=VMEM_LIMIT),
    )(
        pltpu.with_memory_space_constraint(owners, pltpu.SMEM),
        pltpu.with_memory_space_constraint(own, pltpu.HBM),
    )
    states = (master, moment, second, stat_left, stat_right, basis_left, basis_right)
    return lax.switch(
        level[0],
        [functools.partial(update, grid, table, room) for room in table.rooms],
        info,
        fetched,
        other,
        step_count,
        *states,
    )


def update(
    grid,
    table,
    room,
    info,
    own,
    other,
    step_count,
    master,
    moment,
    second,
    stat_left,
    stat_right,
    basis_left,
    basis_right,
):
    slots, size = master.shape[:2]
    blocks = own.shape[0]
    rows = size // table.shares
    chain = Chain()
    correction = 1.0 - jnp.power(jnp.float32(0.95), step_count.astype(F32))
    share = shape((table.each, rows, size), BF16)
    group_state = shape((table.each, size, size), F32)
    group_gradient = shape((table.each, size, size), BF16)
    state = shape((slots, size, size), F32)
    plane = [(dm, dd) for dm in range(grid.middle) for dd in range(grid.dp)]
    passes = slots * size**3
    relay = len(plane) == 4 and grid.dp == 2
    cuts = (0, (room + 1) // 2, room) if relay else (0, room)
    pieces = [shape((end - begin, rows, size), BF16) for begin, end in zip(cuts, cuts[1:])]

    def scatter_plane(sent):
        if not relay:
            return [sent[0][0]] + [
                grid.swap(sent[index][0], middle=dm, dp=dd) for index, (dm, dd) in enumerate(plane) if index
            ]
        mine, along_dp, along_middle, across = sent
        first_one = grid.swap(across[0], middle=1)
        first_two = grid.swap(across[1], dp=1)
        middle_one = grid.swap(along_middle[0], middle=1)
        dp_two = grid.swap(along_dp[1], dp=1)
        dp_one, middle_two = chain.call(
            merge_kernel, (), (along_dp[0], along_middle[1], first_one, first_two), pieces
        )
        dp_one, middle_two = grid.swap(dp_one, dp=1), grid.swap(middle_two, middle=1)
        return [mine[0], middle_one, dp_one, mine[1], dp_two, middle_two]

    def gather_plane(held):
        if not relay:
            got = [(grid.swap(held[0], middle=dm, dp=dd), (dm, dd), 0) for dm, dd in plane[1:]]
            return [(held[0], plane[0], 0)], got
        one, two = held
        middle_one, dp_two = grid.swap(one, middle=1), grid.swap(two, dp=1)
        middle_two, dp_one = grid.swap(two, middle=1), grid.swap(one, dp=1)
        across_one, across_two = grid.swap(middle_one, dp=1), grid.swap(dp_two, middle=1)
        early = [(one, (0, 0), 0), (two, (0, 0), 1), (middle_one, (1, 0), 0), (dp_two, (0, 1), 1)]
        late = [(middle_two, (1, 0), 1), (dp_one, (0, 1), 0), (across_one, (1, 1), 0), (across_two, (1, 1), 1)]
        return early, late

    def pack(given):
        arrays = [array for array, _, _ in given]
        entries = sum(array.shape[0] for array in arrays)
        (packed,) = chain.call(pack_kernel, (), arrays, [shape((entries, rows, size), BF16)], moved=1)
        return packed

    def over_high(arrays):
        return [arrays[0]] + [grid.swap(arrays[dh], high=dh) for dh in range(1, grid.high)]

    outs = chain.call(
        functools.partial(spread_kernel, grid, table, cuts), (info,), (own, other), pieces * len(plane)
    )
    count = len(pieces)
    got = scatter_plane([outs[index * count : (index + 1) * count] for index in range(len(plane))])
    rot_old, left_plain, left_turned, right_tall, right_turned = chain.call(
        prepare_kernel,
        (),
        (moment, basis_left, basis_right),
        [
            state,
            shape((slots, size, 2 * size), BF16),
            shape((slots, size, 2 * size), BF16),
            shape((slots, 2 * size, size), BF16),
            shape((slots, 2 * size, 2 * size), BF16),
        ],
        16 * passes,
    )
    outs = chain.call(
        functools.partial(gather_sum_kernel, grid, table, cuts),
        (info,),
        got,
        [share] * grid.high,
        scratch=(pltpu.VMEM((room, rows, size), BF16),),
    )
    (summed,) = chain.call(sum_kernel, (), over_high(outs), [share])
    parts = [summed] + [grid.swap(summed, dp=dd) for dd in range(1, table.shares)]
    gradient, turned, updated = chain.call(
        functools.partial(step_kernel, grid, table),
        (info, correction),
        (*parts, rot_old, second, master, left_plain, left_turned, right_tall, right_turned),
        [group_gradient, group_state, share],
        14 * passes,
    )
    spread = over_high([updated] * grid.high)
    others = [grid.swap(gradient, dp=dg * table.shares) for dg in range(1, table.groups)]
    bases = (stat_left, stat_right, basis_left, basis_right)
    whole = pltpu.HBM((slots, size, size), F32)
    done = chain.call(
        functools.partial(own_kernel, table),
        (info,),
        (gradient, turned, left_plain, *bases),
        [whole] * 3,
        400 * passes,
        scratch=(pltpu.VMEM((3, table.each, size, size), F32), pltpu.SemaphoreType.DMA),
        specs=[HBM] * 3,
    )
    held = chain.call(
        functools.partial(join_kernel, grid, table, cuts),
        (info,),
        (*spread, *others),
        pieces,
        scratch=(pltpu.VMEM((table.length, rows, size), BF16),),
    )
    early, late = gather_plane(held)
    layout = [[(place, cuts[piece], cuts[piece + 1]) for _, place, piece in part] for part in (early, late)]
    packed = [pack(early)]
    others_state = shape(((table.groups - 1) * table.each, size, size), F32)
    new_bases = chain.call(
        functools.partial(others_kernel, table),
        (info,),
        (*others, *bases),
        [others_state] * 2,
        400 * passes,
    )
    packed.append(pack(late))
    across = [grid.swap(array, core=1) for array in packed]
    prepared = (rot_old, second, left_plain, left_turned, right_tall, right_turned)
    weights = pltpu.HBM((blocks, size, size), BF16)
    direction, left_new, right_new, weights_own = chain.call(
        functools.partial(finish_kernel, grid, table, layout),
        (info, correction),
        (*others, *prepared, *new_bases, *packed),
        [whole] * 3 + [weights],
        100 * passes,
        scratch=(pltpu.VMEM(others_state.shape, F32), pltpu.SemaphoreType.DMA),
        specs=[HBM] * 4,
        moved=1,
        reuse=done,
    )
    (weights_all,) = chain.call(
        functools.partial(weights_kernel, grid, table, layout),
        (info,),
        across,
        [weights],
        scratch=(pltpu.SemaphoreType.DMA,),
        specs=[HBM],
        moved=1,
        reuse=(weights_own,),
    )
    return (weights_all, direction, left_new, right_new)


def solution(mesh):
    placed = (
        P(("dp", "owner"), None, None, None),
        P(),
        P(),
        P("owner", None, None),
        P("owner", None, None),
        P("owner", None, None),
        P("owner", None, None),
        P("owner", None, None),
        P("owner", None, None),
        P("owner", None, None),
    )
    return jax.shard_map(
        body,
        mesh=mesh,
        in_specs=placed,
        out_specs=(P(), P("owner", None, None), P("owner", None, None), P("owner", None, None)),
        check_vma=False,
    )
```

```python
import functools
import math

import jax
import jax.numpy as jnp
from jax import lax
from jax.experimental import pallas as pl
from jax.experimental.pallas import tpu as pltpu
from jax.sharding import PartitionSpec as P

NS_ITERS = 6
AXES = ("dp", "owner")
F32 = jnp.float32
BF16 = jnp.bfloat16
VMEM_LIMIT = 48 * 1024 * 1024
VMEM = pl.BlockSpec(memory_space=pltpu.VMEM)
SMEM = pl.BlockSpec(memory_space=pltpu.SMEM)
HBM = pl.BlockSpec(memory_space=pltpu.HBM)


def shape(dims, dtype):
    return jax.ShapeDtypeStruct(dims, dtype)


class Chain:
    def __init__(self):
        self.token = None

    def call(self, kernel, scalars, arrays, outs, flops=0, scratch=(), specs=None, moved=0, reuse=()):
        moved = moved or sum(math.prod(a.shape) * a.dtype.itemsize for a in [*arrays, *outs])
        count = len(scalars) + len(arrays)
        tokens = () if self.token is None else (self.token,)
        kept = count + len(tokens)
        count_in = kept + len(reuse)
        specs = specs or [VMEM] * len(outs)

        def run(*refs):
            refs = list(refs)
            token = refs.pop(count_in + len(outs))
            kernel(*refs[:count], *refs[count_in:])
            token[...] = jnp.zeros_like(token)

        *results, self.token = pl.pallas_call(
            run,
            out_shape=(*outs, shape((8, 128), F32)),
            in_specs=[SMEM] * len(scalars)
            + [VMEM] * len(arrays)
            + [VMEM] * len(tokens)
            + [HBM] * len(reuse),
            out_specs=(*specs, VMEM),
            scratch_shapes=list(scratch),
            input_output_aliases={kept + index: index for index in range(len(reuse))},
            compiler_params=pltpu.CompilerParams(vmem_limit_bytes=VMEM_LIMIT),
            cost_estimate=pl.CostEstimate(flops=flops, bytes_accessed=moved, transcendentals=0),
        )(*(pltpu.with_memory_space_constraint(a, pltpu.SMEM) for a in scalars), *arrays, *tokens, *reuse)
        return results


class Grid:
    def __init__(self, dp_count, owner_count):
        self.dp, self.core = dp_count, 2
        self.high = 4
        self.middle = owner_count // (self.core * self.high)
        self.owners = owner_count

    def place(self):
        owner = lax.axis_index("owner")
        high, rest = lax.div(owner, self.core * self.middle), lax.rem(owner, self.core * self.middle)
        return lax.axis_index("dp"), high, lax.div(rest, self.core), lax.rem(rest, self.core)

    def swap(self, array, dp=0, high=0, middle=0, core=0):
        step = (high * self.middle + middle) * self.core + core
        pairs = [
            (d * self.owners + o, (d ^ dp) * self.owners + (o ^ step))
            for d in range(self.dp)
            for o in range(self.owners)
        ]
        return lax.ppermute(array, AXES, pairs)


def split(value):
    top = value.astype(BF16)
    return top, (value - top.astype(F32)).astype(BF16)


def dot(left, right, dims):
    return lax.dot_general(left, right, (dims, ((), ())), preferred_element_type=F32)


NN = ((1,), (0,))
NT = ((1,), (1,))
TN = ((0,), (0,))


def as_left(value, axis=1):
    return jnp.concatenate(split(value), axis)


def as_right(value):
    half = jnp.concatenate(split(value), 1)
    return jnp.concatenate([half, half], 0)


def product(left, right, dims=NN):
    wide = dot(left, right, dims)
    size = wide.shape[1] // 2
    return wide[:, :size] + wide[:, size:]


def log2(count):
    return count.bit_length() - 1


class Table:
    def __init__(self, grid, slots):
        self.columns = grid.middle * grid.core
        self.groups = math.gcd(slots, grid.dp)
        self.shares = grid.dp // self.groups
        self.each = slots // self.groups
        self.length = grid.high * self.each
        self.rooms = (self.length * 2 // 3, self.length * 3 // 4, self.length)
        self.listed = 0
        self.counts = self.columns * self.groups * self.length
        self.inverse = self.counts + self.columns * self.groups
        self.held = self.inverse + self.length
        self.place = self.held + 1
        self.size = self.place + 4

    def slot(self, info, group, index):
        turn = group + self.groups - lax.rem(info[self.place + 1], self.groups)
        return self.groups * index + lax.rem(turn, self.groups)


def table_kernel(grid, table, owners, source, out, level, fetched, seen, sem):
    copy = pltpu.make_async_copy(source, fetched, sem)
    copy.start()
    place = grid.place()
    for owner in range(grid.owners):
        seen[owner] = 0
    for part in range(table.columns * table.groups):
        out[table.counts + part] = 0
    for at in range(table.length):
        out[table.inverse + at] = -1
    column_mine = place[2] * grid.core + place[3]
    mine = column_mine * table.groups + lax.div(place[0], table.shares)

    def step(block, carry):
        owner = owners[block]
        rank = seen[owner]
        seen[owner] = rank + 1
        column, high = owner & (table.columns - 1), owner >> log2(table.columns)
        group, index = (rank + high) & (table.groups - 1), rank >> log2(table.groups)
        part = column * table.groups + group
        at = out[table.counts + part]
        out[table.counts + part] = at + 1
        out[table.listed + part * table.length + at] = block

        @pl.when(part == mine)
        def _():
            out[table.inverse + high * table.each + index] = at

        return carry

    lax.fori_loop(0, owners.shape[0], step, 0, unroll=8)
    out[table.held] = seen[place[1] * table.columns + column_mine]
    most = out[table.counts]
    for part in range(1, table.columns * table.groups):
        most = jnp.maximum(most, out[table.counts + part])
    level[0] = sum((most > room).astype(jnp.int32) for room in table.rooms[:-1])
    for at in range(4):
        out[table.place + at] = place[at]
    copy.wait()


def part_of(grid, table, info, dc, dm, dd):
    column = (info[table.place + 2] ^ dm) * grid.core + (info[table.place + 3] ^ dc)
    dp = info[table.place] ^ dd
    part = column * table.groups + lax.div(dp, table.shares)
    return info[table.counts + part], table.listed + part * table.length, lax.rem(dp, table.shares)


def copy_kernel(source, out):
    out[...] = source[...]


def spread_kernel(grid, table, cuts, info, own, other, *outs):
    rows = own.shape[1] // table.shares
    pieces = len(cuts) - 1
    for index in range(grid.middle * grid.dp):
        count, first, share = part_of(grid, table, info, 0, index // grid.dp, index % grid.dp)
        part = pl.ds(pl.multiple_of(share * rows, rows), rows)
        for piece in range(pieces):
            out = outs[index * pieces + piece]

            def put(at, carry):
                block = info[first + at]
                total = own[block, part].astype(F32) + other[block, part].astype(F32)
                out[at - cuts[piece]] = total.astype(BF16)
                return carry

            lax.fori_loop(cuts[piece], jnp.minimum(count, cuts[piece + 1]), put, 0)


def total_of(arrays, at):
    total = arrays[0][at].astype(F32)
    for array in arrays[1:]:
        total = total + array[at].astype(F32)
    return total.astype(BF16)


def gather_sum_kernel(grid, table, cuts, info, *refs):
    arrays, outs, every = refs[: -1 - grid.high], refs[-1 - grid.high : -1], refs[-1]
    each = len(arrays) // (len(cuts) - 1)
    for piece, (begin, end) in enumerate(zip(cuts, cuts[1:])):
        for at in range(begin, end):
            every[at] = total_of(arrays[piece * each : (piece + 1) * each], at - begin)
    for dh in range(grid.high):
        first = table.inverse + (info[table.place + 1] ^ dh) * table.each
        for index in range(table.each):
            outs[dh][index] = every[jnp.clip(info[first + index], 0, cuts[-1] - 1)]


def merge_kernel(*refs):
    count = len(refs) // 3
    for one, two, out in zip(refs[:count], refs[count : 2 * count], refs[2 * count :], strict=True):
        for at in range(out.shape[0]):
            out[at] = total_of((one, two), at)


def sum_kernel(*refs):
    arrays, out = refs[:-1], refs[-1]
    for slot in range(out.shape[0]):
        out[slot] = total_of(arrays, slot)


def prepare_kernel(moment, left, right, rot_old, left_plain, left_turned, right_tall, right_turned):
    for slot in range(rot_old.shape[0]):
        left_t, right_t = left[slot].T, right[slot].T
        half = product(as_left(moment[slot]), as_right(right[slot]))
        left_turned[slot] = as_left(left_t)
        rot_old[slot] = product(as_left(left_t), as_right(half))
        left_plain[slot] = as_left(left[slot])
        right_tall[slot] = as_left(right[slot], 0)
        right_turned[slot] = as_right(right_t)


def rotate(gradient, rot_old, second, left_turned, right_tall, right_turned, c, pairs):
    halves = [dot(jnp.concatenate([gradient[i]] * 2, 1), right_tall[slot], NN) for i, slot in pairs]
    rotated = [
        product(left_turned[slot], as_right(half)) for half, (_, slot) in zip(halves, pairs, strict=True)
    ]
    turned = []
    for value, (_, slot) in zip(rotated, pairs, strict=True):
        rot_moment = 0.95 * rot_old[slot] + 0.05 * value
        second_new = 0.95 * second[slot] + 0.05 * value * value
        scaled = rot_moment / c / (jnp.sqrt(second_new / c) + 1e-08)
        turned.append(product(as_left(scaled), right_turned[slot]))
    return turned


def step_kernel(grid, table, info, correction, *refs):
    parts = refs[: table.shares]
    (rot_old, second, master, left_plain, left_turned, right_tall, right_turned) = refs[table.shares : -3]
    gradient, turned, updated = refs[-3:]
    rows = parts[0].shape[1]
    dp = info[table.place]
    group, share = lax.div(dp, table.shares), lax.rem(dp, table.shares)
    for dd in range(table.shares):
        gradient[:, pl.ds(pl.multiple_of((share ^ dd) * rows, rows), rows), :] = parts[dd][...]
    mine = pl.ds(pl.multiple_of(share * rows, rows), rows)
    pairs = [(index, table.slot(info, group, index)) for index in range(table.each)]
    values = rotate(
        gradient, rot_old, second, left_turned, right_tall, right_turned, correction[0], pairs
    )
    for value, (index, slot) in zip(values, pairs, strict=True):
        turned[index] = value
        weights = master[slot, mine]
        moved = product(left_plain[slot, mine], as_right(value))
        moved = jnp.where(slot < info[table.held], moved, 0.0)
        updated[index] = (weights - 0.01 * (moved + 0.1 * weights)).astype(BF16)


def refresh(gradient, left_stat, right_stat, left, right, pairs):
    iterates = []
    for dims, stat, basis in ((NT, left_stat, left), (TN, right_stat, right)):
        for index, slot in pairs:
            gram = dot(gradient[index], gradient[index], dims)
            power = product(as_left(0.95 * stat[slot] + 0.05 * gram), as_right(basis[slot]))
            iterates.append(power / (jnp.sqrt(jnp.sum(power * power)) + 1e-06))
    for _ in range(NS_ITERS):
        squares = [product(as_left(x, 0), as_right(x), TN) for x in iterates]
        iterates = [
            1.5 * x - 0.5 * product(as_left(x), as_right(square))
            for x, square in zip(iterates, squares, strict=True)
        ]
    return iterates[: len(pairs)], iterates[len(pairs) :]


def own_kernel(table, info, gradient, turned, left_plain, stat_left, stat_right, left, right, *refs):
    outs, (held, sem) = refs[:3], refs[3:]
    group = lax.div(info[table.place], table.shares)
    pairs = [(index, table.slot(info, group, index)) for index in range(table.each)]
    new_left, new_right = refresh(gradient, stat_left, stat_right, left, right, pairs)
    copies = []
    for index, slot in pairs:
        live = slot < info[table.held]
        moved = product(left_plain[slot], as_right(turned[index]))
        held[0, index] = jnp.where(live, moved, 0.0)
        held[1, index] = jnp.where(live, new_left[index], left[slot])
        held[2, index] = jnp.where(live, new_right[index], right[slot])
        copies += [pltpu.make_async_copy(held.at[n, index], outs[n].at[slot], sem) for n in range(3)]
    for copy in copies:
        copy.start()
    for copy in copies:
        copy.wait()


def others_kernel(table, info, *refs):
    count = table.groups - 1
    gradients, bases, (left_out, right_out) = refs[:count], refs[count : count + 4], refs[-2:]
    group = lax.div(info[table.place], table.shares)
    for dg, gradient in enumerate(gradients, 1):
        pairs = [(index, table.slot(info, group ^ dg, index)) for index in range(table.each)]
        new_left, new_right = refresh(gradient, *bases, pairs)
        for index, slot in pairs:
            at = (dg - 1) * table.each + index
            live = slot < info[table.held]
            left_out[at] = jnp.where(live, new_left[index], bases[2][slot])
            right_out[at] = jnp.where(live, new_right[index], bases[3][slot])


def finish_kernel(grid, table, layout, info, correction, *refs):
    count = table.groups - 1
    gradients, refs = refs[:count], refs[count:]
    (rot_old, second, left_plain, left_turned, right_tall, right_turned) = refs[:6]
    new_left, new_right, across, *packed = refs[6 : 9 + len(layout)]
    direction, left_out, right_out, weights, held, sem = refs[9 + len(layout) :]

    def place(act):
        place_blocks(grid, table, layout[:1], 1, info, [across], weights, sem, act)
        place_blocks(grid, table, layout, 0, info, packed, weights, sem, act)

    place(lambda copy: copy.start())
    group = lax.div(info[table.place], table.shares)
    every = [
        (dg, index, table.slot(info, group ^ dg, index))
        for dg in range(1, table.groups)
        for index in range(table.each)
    ]
    copies = []
    for at, (_, _, slot) in enumerate(every):
        copies.append(pltpu.make_async_copy(new_left.at[at], left_out.at[slot], sem))
        copies.append(pltpu.make_async_copy(new_right.at[at], right_out.at[slot], sem))
    for copy in copies:
        copy.start()
    for dg, gradient in enumerate(gradients, 1):
        pairs = [(index, slot) for owner, index, slot in every if owner == dg]
        turned = rotate(
            gradient, rot_old, second, left_turned, right_tall, right_turned, correction[0], pairs
        )
        for index, slot in pairs:
            moved = product(left_plain[slot], as_right(turned[index]))
            at = (dg - 1) * table.each + index
            held[at] = jnp.where(slot < info[table.held], moved, 0.0)
            copies.append(pltpu.make_async_copy(held.at[at], direction.at[slot], sem))
            copies[-1].start()
    for copy in copies:
        copy.wait()
    place(lambda copy: copy.wait())


def join_kernel(grid, table, cuts, info, *refs):
    pieces = len(cuts) - 1
    outs, every = refs[-1 - pieces : -1], refs[-1]
    arrays = dict(zip((1, 2, 3, 0), refs))
    spare = info[table.counts + part_index(grid, table, info)]
    for dh in range(grid.high):
        first = table.inverse + (info[table.place + 1] ^ dh) * table.each
        for index in range(table.each):
            at = info[first + index]
            every[jnp.where(at < 0, spare, at)] = arrays[dh][index]
            spare = spare + (at < 0).astype(jnp.int32)
    for out, begin, end in zip(outs, cuts, cuts[1:]):
        out[...] = every[begin:end]


def pack_kernel(*refs):
    arrays, out = refs[:-1], refs[-1]
    begin = 0
    for array in arrays:
        out[begin : begin + array.shape[0]] = array[...]
        begin += array.shape[0]


def part_index(grid, table, info):
    column = info[table.place + 2] * grid.core + info[table.place + 3]
    return column * table.groups + lax.div(info[table.place], table.shares)


def place_blocks(grid, table, layout, core, info, packed, out, sem, act):
    rows = out.shape[1] // table.shares
    for array, pieces in zip(packed, layout, strict=True):
        base = 0
        for (dm, dd), begin, end in pieces:
            count, first, share = part_of(grid, table, info, core, dm, dd)
            part = pl.ds(pl.multiple_of(share * rows, rows), rows)

            def put(at, carry):
                source = array.at[base - begin + at]
                act(pltpu.make_async_copy(source, out.at[info[first + at], part], sem))
                return carry

            lax.fori_loop(begin, jnp.minimum(count, end), put, 0)
            base += end - begin


def weights_kernel(grid, table, layout, info, *refs):
    packed, (out, sem) = refs[:-2], refs[-2:]
    for act in (lambda copy: copy.start(), lambda copy: copy.wait()):
        place_blocks(grid, table, layout, 1, info, packed, out, sem, act)


def body(
    partials,
    owners,
    step_count,
    master,
    moment,
    second,
    stat_left,
    stat_right,
    basis_left,
    basis_right,
):
    grid = Grid(lax.axis_size("dp"), lax.axis_size("owner"))
    table = Table(grid, master.shape[0])
    own = partials[0]
    other = grid.swap(own, core=1)
    info, level, fetched = pl.pallas_call(
        functools.partial(table_kernel, grid, table),
        out_shape=(
            pltpu.SMEM((table.size,), jnp.int32),
            pltpu.SMEM((1,), jnp.int32),
            pltpu.VMEM(own.shape, BF16),
        ),
        in_specs=[SMEM, HBM],
        out_specs=(SMEM, SMEM, VMEM),
        scratch_shapes=[pltpu.SMEM((grid.owners,), jnp.int32), pltpu.SemaphoreType.DMA],
        compiler_params=pltpu.CompilerParams(vmem_limit_bytes=VMEM_LIMIT),
    )(
        pltpu.with_memory_space_constraint(owners, pltpu.SMEM),
        pltpu.with_memory_space_constraint(own, pltpu.HBM),
    )
    states = (master, moment, second, stat_left, stat_right, basis_left, basis_right)
    return lax.switch(
        level[0],
        [functools.partial(update, grid, table, room) for room in table.rooms],
        info,
        fetched,
        other,
        step_count,
        *states,
    )


def update(
    grid,
    table,
    room,
    info,
    own,
    other,
    step_count,
    master,
    moment,
    second,
    stat_left,
    stat_right,
    basis_left,
    basis_right,
):
    slots, size = master.shape[:2]
    blocks = own.shape[0]
    rows = size // table.shares
    chain = Chain()
    correction = 1.0 - jnp.power(jnp.float32(0.95), step_count.astype(F32))
    share = shape((table.each, rows, size), BF16)
    group_state = shape((table.each, size, size), F32)
    group_gradient = shape((table.each, size, size), BF16)
    state = shape((slots, size, size), F32)
    plane = [(dm, dd) for dm in range(grid.middle) for dd in range(grid.dp)]
    passes = slots * size**3
    relay = len(plane) == 4 and grid.dp == 2
    cuts = (0, (room + 1) // 2, room) if relay else (0, room)
    pieces = [shape((end - begin, rows, size), BF16) for begin, end in zip(cuts, cuts[1:])]

    def scatter_plane(sent):
        if not relay:
            return [sent[0][0]] + [
                grid.swap(sent[index][0], middle=dm, dp=dd) for index, (dm, dd) in enumerate(plane) if index
            ]
        mine, along_dp, along_middle, across = sent
        first_one = grid.swap(across[0], middle=1)
        first_two = grid.swap(across[1], dp=1)
        middle_one = grid.swap(along_middle[0], middle=1)
        dp_two = grid.swap(along_dp[1], dp=1)
        dp_one, middle_two = chain.call(
            merge_kernel, (), (along_dp[0], along_middle[1], first_one, first_two), pieces
        )
        dp_one, middle_two = grid.swap(dp_one, dp=1), grid.swap(middle_two, middle=1)
        return [mine[0], middle_one, dp_one, mine[1], dp_two, middle_two]

    def gather_plane(held):
        if not relay:
            got = [(grid.swap(held[0], middle=dm, dp=dd), (dm, dd), 0) for dm, dd in plane[1:]]
            return [(held[0], plane[0], 0)], got
        one, two = held
        middle_one, dp_two = grid.swap(one, middle=1), grid.swap(two, dp=1)
        middle_two, dp_one = grid.swap(two, middle=1), grid.swap(one, dp=1)
        across_one, across_two = grid.swap(middle_one, dp=1), grid.swap(dp_two, middle=1)
        early = [(one, (0, 0), 0), (two, (0, 0), 1), (middle_one, (1, 0), 0), (dp_two, (0, 1), 1)]
        late = [(middle_two, (1, 0), 1), (dp_one, (0, 1), 0), (across_one, (1, 1), 0), (across_two, (1, 1), 1)]
        return early, late

    def pack(given):
        arrays = [array for array, _, _ in given]
        entries = sum(array.shape[0] for array in arrays)
        (packed,) = chain.call(pack_kernel, (), arrays, [shape((entries, rows, size), BF16)], moved=1)
        return packed

    def over_high(arrays):
        return [arrays[0]] + [grid.swap(arrays[dh], high=dh) for dh in range(1, grid.high)]

    outs = chain.call(
        functools.partial(spread_kernel, grid, table, cuts), (info,), (own, other), pieces * len(plane)
    )
    count = len(pieces)
    got = scatter_plane([outs[index * count : (index + 1) * count] for index in range(len(plane))])
    rot_old, left_plain, left_turned, right_tall, right_turned = chain.call(
        prepare_kernel,
        (),
        (moment, basis_left, basis_right),
        [
            state,
            shape((slots, size, 2 * size), BF16),
            shape((slots, size, 2 * size), BF16),
            shape((slots, 2 * size, size), BF16),
            shape((slots, 2 * size, 2 * size), BF16),
        ],
        16 * passes,
    )
    outs = chain.call(
        functools.partial(gather_sum_kernel, grid, table, cuts),
        (info,),
        got,
        [share] * grid.high,
        scratch=(pltpu.VMEM((room, rows, size), BF16),),
    )
    (summed,) = chain.call(sum_kernel, (), [over_high(outs)[dh] for dh in (3, 2, 1, 0)], [share])
    parts = [summed] + [grid.swap(summed, dp=dd) for dd in range(1, table.shares)]
    gradient, turned, updated = chain.call(
        functools.partial(step_kernel, grid, table),
        (info, correction),
        (*parts, rot_old, second, master, left_plain, left_turned, right_tall, right_turned),
        [group_gradient, group_state, share],
        14 * passes,
    )
    spread = over_high([updated] * grid.high)
    others = [grid.swap(gradient, dp=dg * table.shares) for dg in range(1, table.groups)]
    bases = (stat_left, stat_right, basis_left, basis_right)
    whole = pltpu.HBM((slots, size, size), F32)
    done = chain.call(
        functools.partial(own_kernel, table),
        (info,),
        (gradient, turned, left_plain, *bases),
        [whole] * 3,
        400 * passes,
        scratch=(pltpu.VMEM((3, table.each, size, size), F32), pltpu.SemaphoreType.DMA),
        specs=[HBM] * 3,
    )
    held = chain.call(
        functools.partial(join_kernel, grid, table, cuts),
        (info,),
        (*(spread[dh] for dh in (1, 2, 3, 0)), *others),
        pieces,
        scratch=(pltpu.VMEM((table.length, rows, size), BF16),),
    )
    early, late = gather_plane(held)
    layout = [[(place, cuts[piece], cuts[piece + 1]) for _, place, piece in part] for part in (early, late)]
    packed = [pack(early)]
    others_state = shape(((table.groups - 1) * table.each, size, size), F32)
    new_bases = chain.call(
        functools.partial(others_kernel, table),
        (info,),
        (*others, *bases),
        [others_state] * 2,
        400 * passes,
    )
    packed.append(pack(late))
    across = [grid.swap(array, core=1) for array in packed]
    prepared = (rot_old, second, left_plain, left_turned, right_tall, right_turned)
    weights = pltpu.HBM((blocks, size, size), BF16)
    direction, left_new, right_new, weights_own = chain.call(
        functools.partial(finish_kernel, grid, table, layout),
        (info, correction),
        (*others, *prepared, *new_bases, across[0], *packed),
        [whole] * 3 + [weights],
        100 * passes,
        scratch=(pltpu.VMEM(others_state.shape, F32), pltpu.SemaphoreType.DMA),
        specs=[HBM] * 4,
        moved=1,
        reuse=done,
    )
    (weights_all,) = chain.call(
        functools.partial(weights_kernel, grid, table, layout[1:]),
        (info,),
        across[1:],
        [weights],
        scratch=(pltpu.SemaphoreType.DMA,),
        specs=[HBM],
        moved=1,
        reuse=(weights_own,),
    )
    return (weights_all, direction, left_new, right_new)


def solution(mesh):
    placed = (
        P(("dp", "owner"), None, None, None),
        P(),
        P(),
        P("owner", None, None),
        P("owner", None, None),
        P("owner", None, None),
        P("owner", None, None),
        P("owner", None, None),
        P("owner", None, None),
        P("owner", None, None),
    )
    return jax.shard_map(
        body,
        mesh=mesh,
        in_specs=placed,
        out_specs=(P(), P("owner", None, None), P("owner", None, None), P("owner", None, None)),
        check_vma=False,
    )
```

```python
import functools
import math

import jax
import jax.numpy as jnp
from jax import lax
from jax.experimental import pallas as pl
from jax.experimental.pallas import tpu as pltpu
from jax.sharding import PartitionSpec as P

NS_ITERS = 6
AXES = ("dp", "owner")
F32 = jnp.float32
BF16 = jnp.bfloat16
VMEM_LIMIT = 48 * 1024 * 1024
VMEM = pl.BlockSpec(memory_space=pltpu.VMEM)
SMEM = pl.BlockSpec(memory_space=pltpu.SMEM)
HBM = pl.BlockSpec(memory_space=pltpu.HBM)


def shape(dims, dtype):
    return jax.ShapeDtypeStruct(dims, dtype)


class Chain:
    def __init__(self):
        self.token = None

    def call(self, kernel, scalars, arrays, outs, flops=0, scratch=(), specs=None, moved=0, reuse=()):
        moved = moved or sum(math.prod(a.shape) * a.dtype.itemsize for a in [*arrays, *outs])
        count = len(scalars) + len(arrays)
        tokens = () if self.token is None else (self.token,)
        kept = count + len(tokens)
        count_in = kept + len(reuse)
        specs = specs or [VMEM] * len(outs)

        def run(*refs):
            refs = list(refs)
            token = refs.pop(count_in + len(outs))
            kernel(*refs[:count], *refs[count_in:])
            token[...] = jnp.zeros_like(token)

        *results, self.token = pl.pallas_call(
            run,
            out_shape=(*outs, shape((8, 128), F32)),
            in_specs=[SMEM] * len(scalars)
            + [VMEM] * len(arrays)
            + [VMEM] * len(tokens)
            + [HBM] * len(reuse),
            out_specs=(*specs, VMEM),
            scratch_shapes=list(scratch),
            input_output_aliases={kept + index: index for index in range(len(reuse))},
            compiler_params=pltpu.CompilerParams(vmem_limit_bytes=VMEM_LIMIT),
            cost_estimate=pl.CostEstimate(flops=flops, bytes_accessed=moved, transcendentals=0),
        )(*(pltpu.with_memory_space_constraint(a, pltpu.SMEM) for a in scalars), *arrays, *tokens, *reuse)
        return results


class Grid:
    def __init__(self, dp_count, owner_count):
        self.dp, self.core = dp_count, 2
        self.high = 4
        self.middle = owner_count // (self.core * self.high)
        self.owners = owner_count

    def place(self):
        owner = lax.axis_index("owner")
        high, rest = lax.div(owner, self.core * self.middle), lax.rem(owner, self.core * self.middle)
        return lax.axis_index("dp"), high, lax.div(rest, self.core), lax.rem(rest, self.core)

    def swap(self, array, dp=0, high=0, middle=0, core=0):
        step = (high * self.middle + middle) * self.core + core
        pairs = [
            (d * self.owners + o, (d ^ dp) * self.owners + (o ^ step))
            for d in range(self.dp)
            for o in range(self.owners)
        ]
        return lax.ppermute(array, AXES, pairs)


def split(value):
    top = value.astype(BF16)
    return top, (value - top.astype(F32)).astype(BF16)


def dot(left, right, dims):
    return lax.dot_general(left, right, (dims, ((), ())), preferred_element_type=F32)


NN = ((1,), (0,))
NT = ((1,), (1,))
TN = ((0,), (0,))


def as_left(value, axis=1):
    return jnp.concatenate(split(value), axis)


def as_right(value):
    half = jnp.concatenate(split(value), 1)
    return jnp.concatenate([half, half], 0)


def product(left, right, dims=NN):
    wide = dot(left, right, dims)
    size = wide.shape[1] // 2
    return wide[:, :size] + wide[:, size:]


def log2(count):
    return count.bit_length() - 1


class Table:
    def __init__(self, grid, slots):
        self.columns = grid.middle * grid.core
        self.groups = math.gcd(slots, grid.dp)
        self.shares = grid.dp // self.groups
        self.each = slots // self.groups
        self.length = grid.high * self.each
        self.rooms = (self.length * 2 // 3, self.length * 3 // 4, self.length)
        self.listed = 0
        self.counts = self.columns * self.groups * self.length
        self.inverse = self.counts + self.columns * self.groups
        self.held = self.inverse + self.length
        self.turn = self.held + 1
        self.place = self.turn + 1
        self.size = self.place + 4

    def slot(self, info, group, index):
        return self.groups * index + lax.rem(group + info[self.turn], self.groups)


def table_kernel(grid, table, owners, source, out, level, fetched, seen, turns, sem):
    copy = pltpu.make_async_copy(source, fetched, sem)
    copy.start()
    place = grid.place()
    for owner in range(grid.owners):
        seen[owner] = 0
    for part in range(table.columns * table.groups):
        out[table.counts + part] = 0
    for at in range(table.length):
        out[table.inverse + at] = -1
    column_mine = place[2] * grid.core + place[3]
    mine = column_mine * table.groups + lax.div(place[0], table.shares)

    def count(block, carry):
        owner = owners[block]
        seen[owner] = seen[owner] + 1
        return carry

    lax.fori_loop(0, owners.shape[0], count, 0, unroll=8)
    out[table.held] = seen[place[1] * table.columns + column_mine]
    for column in range(table.columns):
        turn = 0
        for high in range(grid.high):
            owner = high * table.columns + column
            turns[owner] = turn
            turn = (turn + seen[owner]) & (table.groups - 1)
            seen[owner] = 0
    out[table.turn] = (table.groups - turns[place[1] * table.columns + column_mine]) & (table.groups - 1)

    def step(block, carry):
        owner = owners[block]
        rank = seen[owner]
        seen[owner] = rank + 1
        column, high = owner & (table.columns - 1), owner >> log2(table.columns)
        group, index = (rank + turns[owner]) & (table.groups - 1), rank >> log2(table.groups)
        part = column * table.groups + group
        at = out[table.counts + part]
        out[table.counts + part] = at + 1
        out[table.listed + part * table.length + at] = block

        @pl.when(part == mine)
        def _():
            out[table.inverse + high * table.each + index] = at

        return carry

    lax.fori_loop(0, owners.shape[0], step, 0, unroll=8)
    most = out[table.counts]
    for part in range(1, table.columns * table.groups):
        most = jnp.maximum(most, out[table.counts + part])
    level[0] = sum((most > room).astype(jnp.int32) for room in table.rooms[:-1])
    for at in range(4):
        out[table.place + at] = place[at]
    copy.wait()


def part_of(grid, table, info, dc, dm, dd):
    column = (info[table.place + 2] ^ dm) * grid.core + (info[table.place + 3] ^ dc)
    dp = info[table.place] ^ dd
    part = column * table.groups + lax.div(dp, table.shares)
    return info[table.counts + part], table.listed + part * table.length, lax.rem(dp, table.shares)


def copy_kernel(source, out):
    out[...] = source[...]


def spread_kernel(grid, table, cuts, info, own, other, *outs):
    rows = own.shape[1] // table.shares
    pieces = len(cuts) - 1
    for index in range(grid.middle * grid.dp):
        count, first, share = part_of(grid, table, info, 0, index // grid.dp, index % grid.dp)
        part = pl.ds(pl.multiple_of(share * rows, rows), rows)
        for piece in range(pieces):
            out = outs[index * pieces + piece]

            def put(at, carry):
                block = info[first + at]
                total = own[block, part].astype(F32) + other[block, part].astype(F32)
                out[at - cuts[piece]] = total.astype(BF16)
                return carry

            lax.fori_loop(cuts[piece], jnp.minimum(count, cuts[piece + 1]), put, 0)


def total_of(arrays, at):
    total = arrays[0][at].astype(F32)
    for array in arrays[1:]:
        total = total + array[at].astype(F32)
    return total.astype(BF16)


def gather_sum_kernel(grid, table, cuts, info, *refs):
    arrays, outs, every = refs[: -1 - grid.high], refs[-1 - grid.high : -1], refs[-1]
    each = len(arrays) // (len(cuts) - 1)
    for piece, (begin, end) in enumerate(zip(cuts, cuts[1:])):
        for at in range(begin, end):
            every[at] = total_of(arrays[piece * each : (piece + 1) * each], at - begin)
    for dh in range(grid.high):
        first = table.inverse + (info[table.place + 1] ^ dh) * table.each
        for index in range(table.each):
            outs[dh][index] = every[jnp.clip(info[first + index], 0, cuts[-1] - 1)]


def merge_kernel(*refs):
    count = len(refs) // 3
    for one, two, out in zip(refs[:count], refs[count : 2 * count], refs[2 * count :], strict=True):
        for at in range(out.shape[0]):
            out[at] = total_of((one, two), at)


def sum_kernel(*refs):
    arrays, out = refs[:-1], refs[-1]
    for slot in range(out.shape[0]):
        out[slot] = total_of(arrays, slot)


def prepare_kernel(moment, left, right, rot_old, left_plain, left_turned, right_tall, right_turned):
    for slot in range(rot_old.shape[0]):
        left_t, right_t = left[slot].T, right[slot].T
        half = product(as_left(moment[slot]), as_right(right[slot]))
        left_turned[slot] = as_left(left_t)
        rot_old[slot] = product(as_left(left_t), as_right(half))
        left_plain[slot] = as_left(left[slot])
        right_tall[slot] = as_left(right[slot], 0)
        right_turned[slot] = as_right(right_t)


def rotate(gradient, rot_old, second, left_turned, right_tall, right_turned, c, pairs):
    halves = [dot(jnp.concatenate([gradient[i]] * 2, 1), right_tall[slot], NN) for i, slot in pairs]
    rotated = [
        product(left_turned[slot], as_right(half)) for half, (_, slot) in zip(halves, pairs, strict=True)
    ]
    turned = []
    for value, (_, slot) in zip(rotated, pairs, strict=True):
        rot_moment = 0.95 * rot_old[slot] + 0.05 * value
        second_new = 0.95 * second[slot] + 0.05 * value * value
        scaled = rot_moment / c / (jnp.sqrt(second_new / c) + 1e-08)
        turned.append(product(as_left(scaled), right_turned[slot]))
    return turned


def step_kernel(grid, table, info, correction, *refs):
    parts = refs[: table.shares]
    (rot_old, second, master, left_plain, left_turned, right_tall, right_turned) = refs[table.shares : -3]
    gradient, turned, updated = refs[-3:]
    rows = parts[0].shape[1]
    dp = info[table.place]
    group, share = lax.div(dp, table.shares), lax.rem(dp, table.shares)
    for dd in range(table.shares):
        gradient[:, pl.ds(pl.multiple_of((share ^ dd) * rows, rows), rows), :] = parts[dd][...]
    mine = pl.ds(pl.multiple_of(share * rows, rows), rows)
    pairs = [(index, table.slot(info, group, index)) for index in range(table.each)]
    values = rotate(
        gradient, rot_old, second, left_turned, right_tall, right_turned, correction[0], pairs
    )
    for value, (index, slot) in zip(values, pairs, strict=True):
        turned[index] = value
        weights = master[slot, mine]
        moved = product(left_plain[slot, mine], as_right(value))
        moved = jnp.where(slot < info[table.held], moved, 0.0)
        updated[index] = (weights - 0.01 * (moved + 0.1 * weights)).astype(BF16)


def refresh(short, gradient, left_stat, right_stat, left, right, pairs):
    iterates = []
    for dims, stat, basis in ((NT, left_stat, left), (TN, right_stat, right)):
        for index, slot in pairs:
            gram = dot(gradient[index], gradient[index], dims)
            power = product(as_left(0.95 * stat[slot] + 0.05 * gram), as_right(basis[slot]))
            iterates.append(power / (jnp.sqrt(jnp.sum(power * power)) + 1e-06))

    def step(_, iterates):
        squares = [product(as_left(x, 0), as_right(x), TN) for x in iterates]
        return [
            1.5 * x - 0.5 * product(as_left(x), as_right(square))
            for x, square in zip(iterates, squares, strict=True)
        ]

    iterates = lax.fori_loop(0, NS_ITERS, step, iterates, unroll=1 if short else NS_ITERS)
    return iterates[: len(pairs)], iterates[len(pairs) :]


def own_kernel(table, short, info, gradient, turned, left_plain, stat_left, stat_right, left, right, *refs):
    outs, (held, sem) = refs[:3], refs[3:]
    group = lax.div(info[table.place], table.shares)
    pairs = [(index, table.slot(info, group, index)) for index in range(table.each)]
    new_left, new_right = refresh(short, gradient, stat_left, stat_right, left, right, pairs)
    copies = []
    for index, slot in pairs:
        live = slot < info[table.held]
        moved = product(left_plain[slot], as_right(turned[index]))
        held[0, index] = jnp.where(live, moved, 0.0)
        held[1, index] = jnp.where(live, new_left[index], left[slot])
        held[2, index] = jnp.where(live, new_right[index], right[slot])
        copies += [pltpu.make_async_copy(held.at[n, index], outs[n].at[slot], sem) for n in range(3)]
    for copy in copies:
        copy.start()
    for copy in copies:
        copy.wait()


def others_kernel(grid, table, layout, short, info, *refs):
    count = table.groups - 1
    gradients, bases, packed = refs[:count], refs[count : count + 4], refs[count + 4]
    weights, left_out, right_out, sem = refs[-4:]

    def place(act):
        place_blocks(grid, table, layout, 0, info, [packed], weights, sem, act)

    place(lambda copy: copy.start())
    group = lax.div(info[table.place], table.shares)
    for dg, gradient in enumerate(gradients, 1):
        pairs = [(index, table.slot(info, group ^ dg, index)) for index in range(table.each)]
        new_left, new_right = refresh(short, gradient, *bases, pairs)
        for index, slot in pairs:
            at = (dg - 1) * table.each + index
            live = slot < info[table.held]
            left_out[at] = jnp.where(live, new_left[index], bases[2][slot])
            right_out[at] = jnp.where(live, new_right[index], bases[3][slot])
    place(lambda copy: copy.wait())


def finish_kernel(grid, table, early_layout, layout, info, correction, *refs):
    count = table.groups - 1
    gradients, refs = refs[:count], refs[count:]
    (rot_old, second, left_plain, left_turned, right_tall, right_turned) = refs[:6]
    new_left, new_right, packed, across = refs[6:10]
    direction, left_out, right_out, weights, held, sem = refs[10:]

    def place(act):
        place_blocks(grid, table, layout, 0, info, [packed], weights, sem, act)
        place_blocks(grid, table, early_layout, 1, info, [across], weights, sem, act)

    place(lambda copy: copy.start())
    group = lax.div(info[table.place], table.shares)
    every = [
        (dg, index, table.slot(info, group ^ dg, index))
        for dg in range(1, table.groups)
        for index in range(table.each)
    ]
    copies = []
    for at, (_, _, slot) in enumerate(every):
        copies.append(pltpu.make_async_copy(new_left.at[at], left_out.at[slot], sem))
        copies.append(pltpu.make_async_copy(new_right.at[at], right_out.at[slot], sem))
    for copy in copies:
        copy.start()
    for dg, gradient in enumerate(gradients, 1):
        pairs = [(index, slot) for owner, index, slot in every if owner == dg]
        turned = rotate(
            gradient, rot_old, second, left_turned, right_tall, right_turned, correction[0], pairs
        )
        for index, slot in pairs:
            moved = product(left_plain[slot], as_right(turned[index]))
            at = (dg - 1) * table.each + index
            held[at] = jnp.where(slot < info[table.held], moved, 0.0)
            copies.append(pltpu.make_async_copy(held.at[at], direction.at[slot], sem))
            copies[-1].start()
    for copy in copies:
        copy.wait()
    place(lambda copy: copy.wait())


def join_kernel(grid, table, cuts, info, *refs):
    pieces = len(cuts) - 1
    outs, every = refs[-1 - pieces : -1], refs[-1]
    arrays = dict(zip((1, 2, 3, 0), refs))
    spare = info[table.counts + part_index(grid, table, info)]
    for dh in range(grid.high):
        first = table.inverse + (info[table.place + 1] ^ dh) * table.each
        for index in range(table.each):
            at = info[first + index]
            every[jnp.where(at < 0, spare, at)] = arrays[dh][index]
            spare = spare + (at < 0).astype(jnp.int32)
    for out, begin, end in zip(outs, cuts, cuts[1:]):
        out[...] = every[begin:end]


def pack_kernel(*refs):
    arrays, out = refs[:-1], refs[-1]
    begin = 0
    for array in arrays:
        out[begin : begin + array.shape[0]] = array[...]
        begin += array.shape[0]


def part_index(grid, table, info):
    column = info[table.place + 2] * grid.core + info[table.place + 3]
    return column * table.groups + lax.div(info[table.place], table.shares)


def place_blocks(grid, table, layout, core, info, packed, out, sem, act):
    rows = out.shape[1] // table.shares
    for array, pieces in zip(packed, layout, strict=True):
        base = 0
        for (dm, dd), begin, end in pieces:
            count, first, share = part_of(grid, table, info, core, dm, dd)
            part = pl.ds(pl.multiple_of(share * rows, rows), rows)

            def put(at, carry):
                source = array.at[base - begin + at]
                act(pltpu.make_async_copy(source, out.at[info[first + at], part], sem))
                return carry

            lax.fori_loop(begin, jnp.minimum(count, end), put, 0)
            base += end - begin


def weights_kernel(grid, table, layout, info, *refs):
    packed, (out, sem) = refs[:-2], refs[-2:]
    for act in (lambda copy: copy.start(), lambda copy: copy.wait()):
        place_blocks(grid, table, layout, 1, info, packed, out, sem, act)


def body(
    partials,
    owners,
    step_count,
    master,
    moment,
    second,
    stat_left,
    stat_right,
    basis_left,
    basis_right,
):
    grid = Grid(lax.axis_size("dp"), lax.axis_size("owner"))
    table = Table(grid, master.shape[0])
    own = partials[0]
    other = grid.swap(own, core=1)
    info, level, fetched = pl.pallas_call(
        functools.partial(table_kernel, grid, table),
        out_shape=(
            pltpu.SMEM((table.size,), jnp.int32),
            pltpu.SMEM((1,), jnp.int32),
            pltpu.VMEM(own.shape, BF16),
        ),
        in_specs=[SMEM, HBM],
        out_specs=(SMEM, SMEM, VMEM),
        scratch_shapes=[pltpu.SMEM((grid.owners,), jnp.int32)] * 2 + [pltpu.SemaphoreType.DMA],
        compiler_params=pltpu.CompilerParams(vmem_limit_bytes=VMEM_LIMIT),
    )(
        pltpu.with_memory_space_constraint(owners, pltpu.SMEM),
        pltpu.with_memory_space_constraint(own, pltpu.HBM),
    )
    states = (master, moment, second, stat_left, stat_right, basis_left, basis_right)
    return lax.switch(
        level[0],
        [functools.partial(update, grid, table, room) for room in table.rooms],
        info,
        fetched,
        other,
        step_count,
        *states,
    )


def update(
    grid,
    table,
    room,
    info,
    own,
    other,
    step_count,
    master,
    moment,
    second,
    stat_left,
    stat_right,
    basis_left,
    basis_right,
):
    slots, size = master.shape[:2]
    blocks = own.shape[0]
    rows = size // table.shares
    short = room > table.rooms[1]
    chain = Chain()
    correction = 1.0 - jnp.power(jnp.float32(0.95), step_count.astype(F32))
    share = shape((table.each, rows, size), BF16)
    group_state = shape((table.each, size, size), F32)
    group_gradient = shape((table.each, size, size), BF16)
    state = shape((slots, size, size), F32)
    plane = [(dm, dd) for dm in range(grid.middle) for dd in range(grid.dp)]
    passes = slots * size**3
    relay = len(plane) == 4 and grid.dp == 2
    cuts = (0, (room + 1) // 2, room) if relay else (0, room)
    pieces = [shape((end - begin, rows, size), BF16) for begin, end in zip(cuts, cuts[1:])]

    def scatter_plane(sent):
        if not relay:
            return [sent[0][0]] + [
                grid.swap(sent[index][0], middle=dm, dp=dd) for index, (dm, dd) in enumerate(plane) if index
            ]
        mine, along_dp, along_middle, across = sent
        first_one = grid.swap(across[0], middle=1)
        first_two = grid.swap(across[1], dp=1)
        middle_one = grid.swap(along_middle[0], middle=1)
        dp_two = grid.swap(along_dp[1], dp=1)
        dp_one, middle_two = chain.call(
            merge_kernel, (), (along_dp[0], along_middle[1], first_one, first_two), pieces
        )
        dp_one, middle_two = grid.swap(dp_one, dp=1), grid.swap(middle_two, middle=1)
        return [mine[0], middle_one, dp_one, mine[1], dp_two, middle_two]

    def gather_plane(held):
        if not relay:
            got = [(grid.swap(held[0], middle=dm, dp=dd), (dm, dd), 0) for dm, dd in plane[1:]]
            return [(held[0], plane[0], 0)], got
        one, two = held
        middle_one, dp_two = grid.swap(one, middle=1), grid.swap(two, dp=1)
        middle_two, dp_one = grid.swap(two, middle=1), grid.swap(one, dp=1)
        across_one, across_two = grid.swap(middle_one, dp=1), grid.swap(dp_two, middle=1)
        early = [(one, (0, 0), 0), (two, (0, 0), 1), (middle_one, (1, 0), 0), (dp_two, (0, 1), 1)]
        late = [(middle_two, (1, 0), 1), (dp_one, (0, 1), 0), (across_one, (1, 1), 0), (across_two, (1, 1), 1)]
        return early, late

    def pack(given):
        arrays = [array for array, _, _ in given]
        entries = sum(array.shape[0] for array in arrays)
        (packed,) = chain.call(pack_kernel, (), arrays, [shape((entries, rows, size), BF16)], moved=1)
        return packed

    def over_high(arrays):
        return [arrays[0]] + [grid.swap(arrays[dh], high=dh) for dh in range(1, grid.high)]

    outs = chain.call(
        functools.partial(spread_kernel, grid, table, cuts), (info,), (own, other), pieces * len(plane)
    )
    count = len(pieces)
    got = scatter_plane([outs[index * count : (index + 1) * count] for index in range(len(plane))])
    rot_old, left_plain, left_turned, right_tall, right_turned = chain.call(
        prepare_kernel,
        (),
        (moment, basis_left, basis_right),
        [
            state,
            shape((slots, size, 2 * size), BF16),
            shape((slots, size, 2 * size), BF16),
            shape((slots, 2 * size, size), BF16),
            shape((slots, 2 * size, 2 * size), BF16),
        ],
        16 * passes,
    )
    outs = chain.call(
        functools.partial(gather_sum_kernel, grid, table, cuts),
        (info,),
        got,
        [share] * grid.high,
        scratch=(pltpu.VMEM((room, rows, size), BF16),),
    )
    (summed,) = chain.call(sum_kernel, (), [over_high(outs)[dh] for dh in (3, 2, 1, 0)], [share])
    parts = [summed] + [grid.swap(summed, dp=dd) for dd in range(1, table.shares)]
    gradient, turned, updated = chain.call(
        functools.partial(step_kernel, grid, table),
        (info, correction),
        (*parts, rot_old, second, master, left_plain, left_turned, right_tall, right_turned),
        [group_gradient, group_state, share],
        14 * passes,
    )
    spread = over_high([updated] * grid.high)
    others = [grid.swap(gradient, dp=dg * table.shares) for dg in range(1, table.groups)]
    bases = (stat_left, stat_right, basis_left, basis_right)
    whole = pltpu.HBM((slots, size, size), F32)
    done = chain.call(
        functools.partial(own_kernel, table, short),
        (info,),
        (gradient, turned, left_plain, *bases),
        [whole] * 3,
        400 * passes,
        scratch=(pltpu.VMEM((3, table.each, size, size), F32), pltpu.SemaphoreType.DMA),
        specs=[HBM] * 3,
    )
    held = chain.call(
        functools.partial(join_kernel, grid, table, cuts),
        (info,),
        (*(spread[dh] for dh in (1, 2, 3, 0)), *others),
        pieces,
        scratch=(pltpu.VMEM((table.length, rows, size), BF16),),
    )
    early, late = gather_plane(held)
    early_layout, late_layout = (
        [[(place, cuts[piece], cuts[piece + 1]) for _, place, piece in part]] for part in (early, late)
    )
    early = pack(early)
    others_state = shape(((table.groups - 1) * table.each, size, size), F32)
    weights = pltpu.HBM((blocks, size, size), BF16)
    weights_early, new_left, new_right = chain.call(
        functools.partial(others_kernel, grid, table, early_layout, short),
        (info,),
        (*others, *bases, early),
        [weights, others_state, others_state],
        400 * passes,
        scratch=(pltpu.SemaphoreType.DMA,),
        specs=[HBM, VMEM, VMEM],
    )
    early_across = grid.swap(early, core=1)
    late = pack(late)
    late_across = grid.swap(late, core=1)
    prepared = (rot_old, second, left_plain, left_turned, right_tall, right_turned)
    direction, left_new, right_new, weights_own = chain.call(
        functools.partial(finish_kernel, grid, table, early_layout, late_layout),
        (info, correction),
        (*others, *prepared, new_left, new_right, late, early_across),
        [whole] * 3 + [weights],
        100 * passes,
        scratch=(pltpu.VMEM(others_state.shape, F32), pltpu.SemaphoreType.DMA),
        specs=[HBM] * 4,
        moved=1,
        reuse=(*done, weights_early),
    )
    (weights_all,) = chain.call(
        functools.partial(weights_kernel, grid, table, late_layout),
        (info,),
        (late_across,),
        [weights],
        scratch=(pltpu.SemaphoreType.DMA,),
        specs=[HBM],
        moved=1,
        reuse=(weights_own,),
    )
    return (weights_all, direction, left_new, right_new)


def solution(mesh):
    placed = (
        P(("dp", "owner"), None, None, None),
        P(),
        P(),
        P("owner", None, None),
        P("owner", None, None),
        P("owner", None, None),
        P("owner", None, None),
        P("owner", None, None),
        P("owner", None, None),
        P("owner", None, None),
    )
    return jax.shard_map(
        body,
        mesh=mesh,
        in_specs=placed,
        out_specs=(P(), P("owner", None, None), P("owner", None, None), P("owner", None, None)),
        check_vma=False,
    )
```

```python
import functools
import math

import jax
import jax.numpy as jnp
from jax import lax
from jax.experimental import pallas as pl
from jax.experimental.pallas import tpu as pltpu
from jax.sharding import PartitionSpec as P

NS_ITERS = 6
AXES = ("dp", "owner")
F32 = jnp.float32
BF16 = jnp.bfloat16
VMEM_LIMIT = 48 * 1024 * 1024
VMEM = pl.BlockSpec(memory_space=pltpu.VMEM)
SMEM = pl.BlockSpec(memory_space=pltpu.SMEM)
HBM = pl.BlockSpec(memory_space=pltpu.HBM)


def shape(dims, dtype):
    return jax.ShapeDtypeStruct(dims, dtype)


class Chain:
    def __init__(self):
        self.token = None

    def call(self, kernel, scalars, arrays, outs, flops=0, scratch=(), specs=None, moved=0, reuse=()):
        moved = moved or sum(math.prod(a.shape) * a.dtype.itemsize for a in [*arrays, *outs])
        count = len(scalars) + len(arrays)
        tokens = () if self.token is None else (self.token,)
        kept = count + len(tokens)
        count_in = kept + len(reuse)
        specs = specs or [VMEM] * len(outs)

        def run(*refs):
            refs = list(refs)
            token = refs.pop(count_in + len(outs))
            kernel(*refs[:count], *refs[count_in:])
            token[...] = jnp.zeros_like(token)

        *results, self.token = pl.pallas_call(
            run,
            out_shape=(*outs, shape((8, 128), F32)),
            in_specs=[SMEM] * len(scalars)
            + [VMEM] * len(arrays)
            + [VMEM] * len(tokens)
            + [HBM] * len(reuse),
            out_specs=(*specs, VMEM),
            scratch_shapes=list(scratch),
            input_output_aliases={kept + index: index for index in range(len(reuse))},
            compiler_params=pltpu.CompilerParams(vmem_limit_bytes=VMEM_LIMIT),
            cost_estimate=pl.CostEstimate(flops=flops, bytes_accessed=moved, transcendentals=0),
        )(*(pltpu.with_memory_space_constraint(a, pltpu.SMEM) for a in scalars), *arrays, *tokens, *reuse)
        return results


class Grid:
    def __init__(self, dp_count, owner_count):
        self.dp, self.core = dp_count, 2
        self.high = 4
        self.middle = owner_count // (self.core * self.high)
        self.owners = owner_count

    def place(self):
        owner = lax.axis_index("owner")
        high, rest = lax.div(owner, self.core * self.middle), lax.rem(owner, self.core * self.middle)
        return lax.axis_index("dp"), high, lax.div(rest, self.core), lax.rem(rest, self.core)

    def swap(self, array, dp=0, high=0, middle=0, core=0):
        step = (high * self.middle + middle) * self.core + core
        pairs = [
            (d * self.owners + o, (d ^ dp) * self.owners + (o ^ step))
            for d in range(self.dp)
            for o in range(self.owners)
        ]
        return lax.ppermute(array, AXES, pairs)


def split(value):
    top = value.astype(BF16)
    return top, (value - top.astype(F32)).astype(BF16)


def dot(left, right, dims):
    return lax.dot_general(left, right, (dims, ((), ())), preferred_element_type=F32)


NN = ((1,), (0,))
NT = ((1,), (1,))
TN = ((0,), (0,))


def as_left(value, axis=1):
    return jnp.concatenate(split(value), axis)


def as_right(value):
    half = jnp.concatenate(split(value), 1)
    return jnp.concatenate([half, half], 0)


def product(left, right, dims=NN):
    wide = dot(left, right, dims)
    size = wide.shape[1] // 2
    return wide[:, :size] + wide[:, size:]


def log2(count):
    return count.bit_length() - 1


class Table:
    def __init__(self, grid, slots):
        self.columns = grid.middle * grid.core
        self.groups = math.gcd(slots, grid.dp)
        self.shares = grid.dp // self.groups
        self.each = slots // self.groups
        self.length = grid.high * self.each
        self.rooms = (self.length * 2 // 3, self.length * 3 // 4, self.length)
        self.listed = 0
        self.counts = self.columns * self.groups * self.length
        self.inverse = self.counts + self.columns * self.groups
        self.held = self.inverse + self.length
        self.turn = self.held + 1
        self.place = self.turn + 1
        self.size = self.place + 4

    def slot(self, info, group, index):
        return self.groups * index + lax.rem(group + info[self.turn], self.groups)


def table_kernel(grid, table, owners, source, out, level, fetched, seen, turns, sem):
    copy = pltpu.make_async_copy(source, fetched, sem)
    copy.start()
    place = grid.place()
    for owner in range(grid.owners):
        seen[owner] = 0
    for part in range(table.columns * table.groups):
        out[table.counts + part] = 0
    for at in range(table.length):
        out[table.inverse + at] = -1
    column_mine = place[2] * grid.core + place[3]
    mine = column_mine * table.groups + lax.div(place[0], table.shares)

    def count(block, carry):
        owner = owners[block]
        seen[owner] = seen[owner] + 1
        return carry

    lax.fori_loop(0, owners.shape[0], count, 0, unroll=8)
    out[table.held] = seen[place[1] * table.columns + column_mine]
    for column in range(table.columns):
        turn = 0
        for high in range(grid.high):
            owner = high * table.columns + column
            turns[owner] = turn
            turn = (turn + seen[owner]) & (table.groups - 1)
            seen[owner] = 0
    out[table.turn] = (table.groups - turns[place[1] * table.columns + column_mine]) & (table.groups - 1)

    def step(block, carry):
        owner = owners[block]
        rank = seen[owner]
        seen[owner] = rank + 1
        column, high = owner & (table.columns - 1), owner >> log2(table.columns)
        group, index = (rank + turns[owner]) & (table.groups - 1), rank >> log2(table.groups)
        part = column * table.groups + group
        at = out[table.counts + part]
        out[table.counts + part] = at + 1
        out[table.listed + part * table.length + at] = block

        @pl.when(part == mine)
        def _():
            out[table.inverse + high * table.each + index] = at

        return carry

    lax.fori_loop(0, owners.shape[0], step, 0, unroll=8)
    most = out[table.counts]
    for part in range(1, table.columns * table.groups):
        most = jnp.maximum(most, out[table.counts + part])
    level[0] = sum((most > room).astype(jnp.int32) for room in table.rooms[:-1])
    for at in range(4):
        out[table.place + at] = place[at]
    copy.wait()


def part_of(grid, table, info, dc, dm, dd):
    column = (info[table.place + 2] ^ dm) * grid.core + (info[table.place + 3] ^ dc)
    dp = info[table.place] ^ dd
    part = column * table.groups + lax.div(dp, table.shares)
    return info[table.counts + part], table.listed + part * table.length, lax.rem(dp, table.shares)


def copy_kernel(source, out):
    out[...] = source[...]


def spread_kernel(grid, table, cuts, info, own, other, *outs):
    rows = own.shape[1] // table.shares
    pieces = len(cuts) - 1
    for index in range(grid.middle * grid.dp):
        count, first, share = part_of(grid, table, info, 0, index // grid.dp, index % grid.dp)
        part = pl.ds(pl.multiple_of(share * rows, rows), rows)
        for piece in range(pieces):
            out = outs[index * pieces + piece]

            def put(at, carry):
                block = info[first + at]
                total = own[block, part].astype(F32) + other[block, part].astype(F32)
                out[at - cuts[piece]] = total.astype(BF16)
                return carry

            lax.fori_loop(cuts[piece], jnp.minimum(count, cuts[piece + 1]), put, 0)


def total_of(arrays, at):
    total = arrays[0][at].astype(F32)
    for array in arrays[1:]:
        total = total + array[at].astype(F32)
    return total.astype(BF16)


def gather_sum_kernel(grid, table, cuts, info, *refs):
    arrays, outs, every = refs[: -1 - grid.high], refs[-1 - grid.high : -1], refs[-1]
    each = len(arrays) // (len(cuts) - 1)
    for piece, (begin, end) in enumerate(zip(cuts, cuts[1:])):
        for at in range(begin, end):
            every[at] = total_of(arrays[piece * each : (piece + 1) * each], at - begin)
    for dh in range(grid.high):
        first = table.inverse + (info[table.place + 1] ^ dh) * table.each
        for index in range(table.each):
            outs[dh][index] = every[jnp.clip(info[first + index], 0, cuts[-1] - 1)]


def merge_kernel(*refs):
    count = len(refs) // 3
    for one, two, out in zip(refs[:count], refs[count : 2 * count], refs[2 * count :], strict=True):
        for at in range(out.shape[0]):
            out[at] = total_of((one, two), at)


def sum_kernel(*refs):
    arrays, out = refs[:-1], refs[-1]
    for slot in range(out.shape[0]):
        out[slot] = total_of(arrays, slot)


def prepare_kernel(moment, left, right, rot_old, left_plain, left_turned, right_tall, right_turned):
    for slot in range(rot_old.shape[0]):
        left_t, right_t = left[slot].T, right[slot].T
        half = product(as_left(moment[slot]), as_right(right[slot]))
        left_turned[slot] = as_left(left_t)
        rot_old[slot] = product(as_left(left_t), as_right(half))
        left_plain[slot] = as_left(left[slot])
        right_tall[slot] = as_left(right[slot], 0)
        right_turned[slot] = as_right(right_t)


def rotate(gradient, rot_old, second, left_turned, right_tall, right_turned, c, pairs):
    halves = [dot(jnp.concatenate([gradient[i]] * 2, 1), right_tall[slot], NN) for i, slot in pairs]
    rotated = [
        product(left_turned[slot], as_right(half)) for half, (_, slot) in zip(halves, pairs, strict=True)
    ]
    turned = []
    for value, (_, slot) in zip(rotated, pairs, strict=True):
        rot_moment = 0.95 * rot_old[slot] + 0.05 * value
        second_new = 0.95 * second[slot] + 0.05 * value * value
        scaled = rot_moment / c / (jnp.sqrt(second_new / c) + 1e-08)
        turned.append(product(as_left(scaled), right_turned[slot]))
    return turned


def step_kernel(grid, table, info, correction, *refs):
    parts = refs[: table.shares]
    (rot_old, second, master, left_plain, left_turned, right_tall, right_turned) = refs[table.shares : -3]
    gradient, turned, updated = refs[-3:]
    rows = parts[0].shape[1]
    dp = info[table.place]
    group, share = lax.div(dp, table.shares), lax.rem(dp, table.shares)
    for dd in range(table.shares):
        gradient[:, pl.ds(pl.multiple_of((share ^ dd) * rows, rows), rows), :] = parts[dd][...]
    mine = pl.ds(pl.multiple_of(share * rows, rows), rows)
    pairs = [(index, table.slot(info, group, index)) for index in range(table.each)]
    values = rotate(
        gradient, rot_old, second, left_turned, right_tall, right_turned, correction[0], pairs
    )
    for value, (index, slot) in zip(values, pairs, strict=True):
        turned[index] = value
        weights = master[slot, mine]
        moved = product(left_plain[slot, mine], as_right(value))
        moved = jnp.where(slot < info[table.held], moved, 0.0)
        updated[index] = (weights - 0.01 * (moved + 0.1 * weights)).astype(BF16)


def refresh(short, gradient, left_stat, right_stat, left, right, pairs):
    iterates = []
    for dims, stat, basis in ((NT, left_stat, left), (TN, right_stat, right)):
        for index, slot in pairs:
            gram = dot(gradient[index], gradient[index], dims)
            power = product(as_left(0.95 * stat[slot] + 0.05 * gram), as_right(basis[slot]))
            iterates.append(power / (jnp.sqrt(jnp.sum(power * power)) + 1e-06))

    def step(_, iterates):
        squares = [product(as_left(x, 0), as_right(x), TN) for x in iterates]
        return [
            1.5 * x - 0.5 * product(as_left(x), as_right(square))
            for x, square in zip(iterates, squares, strict=True)
        ]

    iterates = lax.fori_loop(0, NS_ITERS, step, iterates, unroll=1 if short else NS_ITERS)
    return iterates[: len(pairs)], iterates[len(pairs) :]


def own_kernel(table, short, info, gradient, turned, left_plain, stat_left, stat_right, left, right, *refs):
    outs, (held, sem) = refs[:3], refs[3:]
    group = lax.div(info[table.place], table.shares)
    pairs = [(index, table.slot(info, group, index)) for index in range(table.each)]
    new_left, new_right = refresh(short, gradient, stat_left, stat_right, left, right, pairs)
    copies = []
    for index, slot in pairs:
        live = slot < info[table.held]
        moved = product(left_plain[slot], as_right(turned[index]))
        held[0, index] = jnp.where(live, moved, 0.0)
        held[1, index] = jnp.where(live, new_left[index], left[slot])
        held[2, index] = jnp.where(live, new_right[index], right[slot])
        copies += [pltpu.make_async_copy(held.at[n, index], outs[n].at[slot], sem) for n in range(3)]
    for copy in copies:
        copy.start()
    for copy in copies:
        copy.wait()


def others_kernel(grid, table, layout, short, info, *refs):
    count = table.groups - 1
    gradients, bases, packed = refs[:count], refs[count : count + 4], refs[count + 4]
    left_out, right_out, weights, held, sem = refs[-5:]
    copies = []

    def place(act):
        place_blocks(grid, table, layout, 0, info, [packed], weights, sem, act)

    place(lambda copy: copy.start())
    group = lax.div(info[table.place], table.shares)
    for dg, gradient in enumerate(gradients, 1):
        pairs = [(index, table.slot(info, group ^ dg, index)) for index in range(table.each)]
        new_left, new_right = refresh(short, gradient, *bases, pairs)
        for index, slot in pairs:
            at = (dg - 1) * table.each + index
            live = slot < info[table.held]
            held[0, at] = jnp.where(live, new_left[index], bases[2][slot])
            held[1, at] = jnp.where(live, new_right[index], bases[3][slot])
            copies.append(pltpu.make_async_copy(held.at[0, at], left_out.at[slot], sem))
            copies.append(pltpu.make_async_copy(held.at[1, at], right_out.at[slot], sem))
    for copy in copies:
        copy.start()
    for copy in copies:
        copy.wait()
    place(lambda copy: copy.wait())


def finish_kernel(grid, table, early_layout, layout, info, correction, *refs):
    count = table.groups - 1
    gradients, refs = refs[:count], refs[count:]
    (rot_old, second, left_plain, left_turned, right_tall, right_turned) = refs[:6]
    packed, across = refs[6:8]
    direction, weights, held, sem = refs[8:]

    def place(act):
        place_blocks(grid, table, layout, 0, info, [packed], weights, sem, act)
        place_blocks(grid, table, early_layout, 1, info, [across], weights, sem, act)

    place(lambda copy: copy.start())
    group = lax.div(info[table.place], table.shares)
    every = [
        (dg, index, table.slot(info, group ^ dg, index))
        for dg in range(1, table.groups)
        for index in range(table.each)
    ]
    copies = []
    for dg, gradient in enumerate(gradients, 1):
        pairs = [(index, slot) for owner, index, slot in every if owner == dg]
        turned = rotate(
            gradient, rot_old, second, left_turned, right_tall, right_turned, correction[0], pairs
        )
        for index, slot in pairs:
            moved = product(left_plain[slot], as_right(turned[index]))
            at = (dg - 1) * table.each + index
            held[at] = jnp.where(slot < info[table.held], moved, 0.0)
            copies.append(pltpu.make_async_copy(held.at[at], direction.at[slot], sem))
            copies[-1].start()
    for copy in copies:
        copy.wait()
    place(lambda copy: copy.wait())


def join_kernel(grid, table, cuts, info, *refs):
    pieces = len(cuts) - 1
    outs, every = refs[-1 - pieces : -1], refs[-1]
    arrays = dict(zip((1, 2, 3, 0), refs))
    spare = info[table.counts + part_index(grid, table, info)]
    for dh in range(grid.high):
        first = table.inverse + (info[table.place + 1] ^ dh) * table.each
        for index in range(table.each):
            at = info[first + index]
            every[jnp.where(at < 0, spare, at)] = arrays[dh][index]
            spare = spare + (at < 0).astype(jnp.int32)
    for out, begin, end in zip(outs, cuts, cuts[1:]):
        out[...] = every[begin:end]


def pack_kernel(*refs):
    arrays, out = refs[:-1], refs[-1]
    begin = 0
    for array in arrays:
        out[begin : begin + array.shape[0]] = array[...]
        begin += array.shape[0]


def part_index(grid, table, info):
    column = info[table.place + 2] * grid.core + info[table.place + 3]
    return column * table.groups + lax.div(info[table.place], table.shares)


def place_blocks(grid, table, layout, core, info, packed, out, sem, act):
    rows = out.shape[1] // table.shares
    for array, pieces in zip(packed, layout, strict=True):
        base = 0
        for (dm, dd), begin, end in pieces:
            count, first, share = part_of(grid, table, info, core, dm, dd)
            part = pl.ds(pl.multiple_of(share * rows, rows), rows)

            def put(at, carry):
                source = array.at[base - begin + at]
                act(pltpu.make_async_copy(source, out.at[info[first + at], part], sem))
                return carry

            lax.fori_loop(begin, jnp.minimum(count, end), put, 0)
            base += end - begin


def weights_kernel(grid, table, layout, info, *refs):
    packed, (out, sem) = refs[:-2], refs[-2:]
    for act in (lambda copy: copy.start(), lambda copy: copy.wait()):
        place_blocks(grid, table, layout, 1, info, packed, out, sem, act)


def body(
    partials,
    owners,
    step_count,
    master,
    moment,
    second,
    stat_left,
    stat_right,
    basis_left,
    basis_right,
):
    grid = Grid(lax.axis_size("dp"), lax.axis_size("owner"))
    table = Table(grid, master.shape[0])
    own = partials[0]
    other = grid.swap(own, core=1)
    info, level, fetched = pl.pallas_call(
        functools.partial(table_kernel, grid, table),
        out_shape=(
            pltpu.SMEM((table.size,), jnp.int32),
            pltpu.SMEM((1,), jnp.int32),
            pltpu.VMEM(own.shape, BF16),
        ),
        in_specs=[SMEM, HBM],
        out_specs=(SMEM, SMEM, VMEM),
        scratch_shapes=[pltpu.SMEM((grid.owners,), jnp.int32)] * 2 + [pltpu.SemaphoreType.DMA],
        compiler_params=pltpu.CompilerParams(vmem_limit_bytes=VMEM_LIMIT),
    )(
        pltpu.with_memory_space_constraint(owners, pltpu.SMEM),
        pltpu.with_memory_space_constraint(own, pltpu.HBM),
    )
    states = (master, moment, second, stat_left, stat_right, basis_left, basis_right)
    return lax.switch(
        level[0],
        [functools.partial(update, grid, table, room) for room in table.rooms],
        info,
        fetched,
        other,
        step_count,
        *states,
    )


def update(
    grid,
    table,
    room,
    info,
    own,
    other,
    step_count,
    master,
    moment,
    second,
    stat_left,
    stat_right,
    basis_left,
    basis_right,
):
    slots, size = master.shape[:2]
    blocks = own.shape[0]
    rows = size // table.shares
    short = room > table.rooms[1]
    chain = Chain()
    correction = 1.0 - jnp.power(jnp.float32(0.95), step_count.astype(F32))
    share = shape((table.each, rows, size), BF16)
    group_state = shape((table.each, size, size), F32)
    group_gradient = shape((table.each, size, size), BF16)
    state = shape((slots, size, size), F32)
    plane = [(dm, dd) for dm in range(grid.middle) for dd in range(grid.dp)]
    passes = slots * size**3
    relay = len(plane) == 4 and grid.dp == 2
    cuts = (0, (room + 1) // 2, room) if relay else (0, room)
    pieces = [shape((end - begin, rows, size), BF16) for begin, end in zip(cuts, cuts[1:])]

    def scatter_plane(sent):
        if not relay:
            return [sent[0][0]] + [
                grid.swap(sent[index][0], middle=dm, dp=dd) for index, (dm, dd) in enumerate(plane) if index
            ]
        mine, along_dp, along_middle, across = sent
        first_one = grid.swap(across[0], middle=1)
        first_two = grid.swap(across[1], dp=1)
        middle_one = grid.swap(along_middle[0], middle=1)
        dp_two = grid.swap(along_dp[1], dp=1)
        dp_one, middle_two = chain.call(
            merge_kernel, (), (along_dp[0], along_middle[1], first_one, first_two), pieces
        )
        dp_one, middle_two = grid.swap(dp_one, dp=1), grid.swap(middle_two, middle=1)
        return [mine[0], middle_one, dp_one, mine[1], dp_two, middle_two]

    def gather_plane(held):
        if not relay:
            got = [(grid.swap(held[0], middle=dm, dp=dd), (dm, dd), 0) for dm, dd in plane[1:]]
            return [(held[0], plane[0], 0)], got
        one, two = held
        middle_one, dp_two = grid.swap(one, middle=1), grid.swap(two, dp=1)
        middle_two, dp_one = grid.swap(two, middle=1), grid.swap(one, dp=1)
        across_one, across_two = grid.swap(middle_one, dp=1), grid.swap(dp_two, middle=1)
        early = [(one, (0, 0), 0), (two, (0, 0), 1), (middle_one, (1, 0), 0), (dp_two, (0, 1), 1)]
        late = [(middle_two, (1, 0), 1), (dp_one, (0, 1), 0), (across_one, (1, 1), 0), (across_two, (1, 1), 1)]
        return early, late

    def pack(given):
        arrays = [array for array, _, _ in given]
        entries = sum(array.shape[0] for array in arrays)
        (packed,) = chain.call(pack_kernel, (), arrays, [shape((entries, rows, size), BF16)], moved=1)
        return packed

    def over_high(arrays):
        return [arrays[0]] + [grid.swap(arrays[dh], high=dh) for dh in range(1, grid.high)]

    outs = chain.call(
        functools.partial(spread_kernel, grid, table, cuts), (info,), (own, other), pieces * len(plane)
    )
    count = len(pieces)
    got = scatter_plane([outs[index * count : (index + 1) * count] for index in range(len(plane))])
    rot_old, left_plain, left_turned, right_tall, right_turned = chain.call(
        prepare_kernel,
        (),
        (moment, basis_left, basis_right),
        [
            state,
            shape((slots, size, 2 * size), BF16),
            shape((slots, size, 2 * size), BF16),
            shape((slots, 2 * size, size), BF16),
            shape((slots, 2 * size, 2 * size), BF16),
        ],
        16 * passes,
    )
    outs = chain.call(
        functools.partial(gather_sum_kernel, grid, table, cuts),
        (info,),
        got,
        [share] * grid.high,
        scratch=(pltpu.VMEM((room, rows, size), BF16),),
    )
    (summed,) = chain.call(sum_kernel, (), [over_high(outs)[dh] for dh in (3, 2, 1, 0)], [share])
    parts = [summed] + [grid.swap(summed, dp=dd) for dd in range(1, table.shares)]
    gradient, turned, updated = chain.call(
        functools.partial(step_kernel, grid, table),
        (info, correction),
        (*parts, rot_old, second, master, left_plain, left_turned, right_tall, right_turned),
        [group_gradient, group_state, share],
        14 * passes,
    )
    spread = over_high([updated] * grid.high)
    others = [grid.swap(gradient, dp=dg * table.shares) for dg in range(1, table.groups)]
    bases = (stat_left, stat_right, basis_left, basis_right)
    whole = pltpu.HBM((slots, size, size), F32)
    done = chain.call(
        functools.partial(own_kernel, table, short),
        (info,),
        (gradient, turned, left_plain, *bases),
        [whole] * 3,
        400 * passes,
        scratch=(pltpu.VMEM((3, table.each, size, size), F32), pltpu.SemaphoreType.DMA),
        specs=[HBM] * 3,
    )
    held = chain.call(
        functools.partial(join_kernel, grid, table, cuts),
        (info,),
        (*(spread[dh] for dh in (1, 2, 3, 0)), *others),
        pieces,
        scratch=(pltpu.VMEM((table.length, rows, size), BF16),),
    )
    early, late = gather_plane(held)
    early_layout, late_layout = (
        [[(place, cuts[piece], cuts[piece + 1]) for _, place, piece in part]] for part in (early, late)
    )
    early = pack(early)
    others_state = shape(((table.groups - 1) * table.each, size, size), F32)
    weights = pltpu.HBM((blocks, size, size), BF16)
    left_new, right_new, weights_early = chain.call(
        functools.partial(others_kernel, grid, table, early_layout, short),
        (info,),
        (*others, *bases, early),
        [whole, whole, weights],
        400 * passes,
        scratch=(pltpu.VMEM((2, *others_state.shape), F32), pltpu.SemaphoreType.DMA),
        specs=[HBM] * 3,
        reuse=done[1:],
    )
    early_across = grid.swap(early, core=1)
    late = pack(late)
    late_across = grid.swap(late, core=1)
    prepared = (rot_old, second, left_plain, left_turned, right_tall, right_turned)
    direction, weights_own = chain.call(
        functools.partial(finish_kernel, grid, table, early_layout, late_layout),
        (info, correction),
        (*others, *prepared, late, early_across),
        [whole, weights],
        100 * passes,
        scratch=(pltpu.VMEM(others_state.shape, F32), pltpu.SemaphoreType.DMA),
        specs=[HBM] * 2,
        moved=1,
        reuse=(done[0], weights_early),
    )
    (weights_all,) = chain.call(
        functools.partial(weights_kernel, grid, table, late_layout),
        (info,),
        (late_across,),
        [weights],
        scratch=(pltpu.SemaphoreType.DMA,),
        specs=[HBM],
        moved=1,
        reuse=(weights_own,),
    )
    return (weights_all, direction, left_new, right_new)


def solution(mesh):
    placed = (
        P(("dp", "owner"), None, None, None),
        P(),
        P(),
        P("owner", None, None),
        P("owner", None, None),
        P("owner", None, None),
        P("owner", None, None),
        P("owner", None, None),
        P("owner", None, None),
        P("owner", None, None),
    )
    return jax.shard_map(
        body,
        mesh=mesh,
        in_specs=placed,
        out_specs=(P(), P("owner", None, None), P("owner", None, None), P("owner", None, None)),
        check_vma=False,
    )
```
